256 devices in a mesh: grp: 2 (over core), beam: 16 (over z, x_lo), tp: 8 (over x_hi, y).
Axes of the slice: x: 4 (x_hi: 2, x_lo: 2; x = x_hi * 2 + x_lo), y: 4, z: 8, core: 2. Of those that a mesh axis runs over, the one named last changes fastest.
Arguments:
- queries: bfloat16 [2, 1024, 4, 8192], P('grp', 'beam', None, 'tp'), may hold values from -128 to 128
- new_kv: bfloat16 [2, 1024, 4, 2048], P('grp', 'beam', None, 'tp'), may hold values from -12 to 12
- prompt_key_value: bfloat16 [2, 2, 4096, 2048], P('grp', None, 'beam', 'tp'), may hold values from -12 to 12
- step_key_value: bfloat16 [2, 1024, 128, 2048], P('grp', 'beam', None, 'tp'), may hold values from -12 to 12
- parent_dev: int32 [1024, 1], replicated, may hold values from 0 to 15; in each aligned block of 64 rows (0 to 63, 64 to 127, ...) at most 8 rows name the same one
- parent_slot: int32 [1024], replicated, may hold values from 0 to 63
- cache_len: int32 [1024], replicated, may hold values from 1 to 128, as said below
- prompt_ids: int32 [1024], P('beam'), may hold values from 0 to 1
- score_weights: float32 [2, 8192], P('grp', 'tp'), may hold values from -0.0625 to 0.0625
Outputs:
- attended: bfloat16 [2, 1024, 4, 8192], P('grp', 'beam', None, 'tp')
- beam_score: float32 [1024], P('beam')
The draws below stay inside these ranges and needn't reach their ends.
Inputs may be any that keep to these rules, and one draw needn't show every extreme that they name: `parent_dev`: among the 64 beams of one device, at most 8 have parents on one device, and this bound is reached. `cache_len`: each device's block of 64 beams holds at least one beam of length 128.
All inputs are finite; a program needn't handle non-finite values.
Results may differ from the reference program's by a relative error of at most 0.0065.
Values may be sent and summed in bfloat16 or wider, within the bound.
A program may use at most 128 MiB of HBM per device.

```python
import math
import jax
import jax.numpy as jnp
import numpy as np
from jax import lax

QUERY_HEADS = 64
KEY_HEADS = 8
HEAD_SIZE = 128
NEW_TOKENS = 4
PROMPT_TOTAL = 2
BEAM_DEV = 64
STEP_LENGTH = 128
HOLDERS = 16
BEAM_TOTAL = 1024
PROMPT_LENGTH = 4096
MOST = 8


def first_keys(key):
    return jnp.clip(2.0 * jax.random.normal(key, (2, BEAM_TOTAL, KEY_HEADS, HEAD_SIZE), jnp.float32), -12.0, 12.0)


def draw_queries(key, part):
    key = jax.random.fold_in(key, 7)
    value_entries = jnp.clip(jax.random.normal(key, (2, BEAM_TOTAL, NEW_TOKENS, KEY_HEADS, QUERY_HEADS // KEY_HEADS, HEAD_SIZE), jnp.float32), -6.0, 6.0)
    return value_entries.reshape(2, BEAM_TOTAL, NEW_TOKENS, QUERY_HEADS * HEAD_SIZE).astype(jnp.bfloat16)


def draw_new_kv(key, part):
    leading = first_keys(key)
    key = jax.random.fold_in(key, 11)
    prompt_key_part, step_key_part = jax.random.split(key)
    key_matrix = jnp.clip(2.0 * jax.random.normal(prompt_key_part, (2, BEAM_TOTAL, NEW_TOKENS, KEY_HEADS, HEAD_SIZE), jnp.float32), -12.0, 12.0)
    key_matrix = key_matrix.at[:, :, 0].set(leading)
    value_matrix = jnp.clip(2.0 * jax.random.normal(step_key_part, (2, BEAM_TOTAL, NEW_TOKENS, KEY_HEADS, HEAD_SIZE), jnp.float32), -12.0, 12.0)
    merged_keys = jnp.stack([key_matrix, value_matrix], axis=4)
    return merged_keys.reshape(2, BEAM_TOTAL, NEW_TOKENS, KEY_HEADS * 2 * HEAD_SIZE).astype(jnp.bfloat16)


def draw_cache_len(key, part):
    key = jax.random.fold_in(key, 5)
    prompt_key_part, step_key_part = jax.random.split(key)
    lengths = jax.random.randint(prompt_key_part, (BEAM_TOTAL,), 1, STEP_LENGTH + 1, dtype=jnp.int32)
    picked = jax.random.randint(step_key_part, (BEAM_TOTAL // BEAM_DEV, 1), 0, BEAM_DEV, dtype=jnp.int32)
    longest = jnp.arange(BEAM_DEV, dtype=jnp.int32)[None, :] == picked
    return jnp.where(longest.reshape(-1), STEP_LENGTH, lengths).astype(jnp.int32)


def with_ends(values, own_key, smallest, largest):
    spot = [jax.random.randint(jax.random.fold_in(own_key, axis), (), 0, length) for axis, length in enumerate(values.shape)]
    main_axis = values.shape.index(max(values.shape))
    next_to = spot[:main_axis] + [(spot[main_axis] + 1) % values.shape[main_axis]] + spot[main_axis + 1:]
    return values.at[tuple(spot)].set(smallest).at[tuple(next_to)].set(largest)


def steps_of(rng, shape, cuts, low, high):
    gain, own = 1.0, jax.random.fold_in(rng, 6)
    for dim, blocks in cuts:
        heights = jnp.exp(jax.random.uniform(jax.random.fold_in(own, dim), (blocks,), jnp.float32, low / len(cuts), high / len(cuts)))
        gain = gain * jnp.repeat(heights, shape[dim] // blocks).reshape([-1 if axis == dim else 1 for axis in range(len(shape))])
    return gain


def rank_bounds(amount, lean):
    portions = [(1 << 20) // math.isqrt(rank ** lean) + 1 for rank in range(1, amount + 1)]
    spread = 1 + sum(portions) // (1 << 30)
    return np.cumsum(np.array([max(1, weight // spread) for weight in portions]))


def skewed_ids(stream_key, shape, number_of, slope):
    listing = rank_bounds(number_of, slope)
    ticket = jax.random.randint(jax.random.fold_in(stream_key, 1), shape, 0, int(listing[number_of - 1]))
    standing = jnp.searchsorted(jnp.asarray(listing, jnp.int32), ticket, side="right")
    return jax.random.permutation(jax.random.fold_in(stream_key, 2), number_of)[standing].astype(jnp.int32)


def assign_block(own_key, own, number, rows, amount, top, limit, slope):
    ranking = jax.random.permutation(own_key, amount)
    crowded, usual = portions_of(amount, rows * top, limit, slope, True), portions_of(amount, rows * top, limit, slope, False)
    places = jnp.arange(amount)

    def named(sizes, turn):
        used = int((sizes > 0).sum())
        fixed = max(1, used // 4)
        shifted = fixed + (places - fixed + turn * (used - fixed)) % max(1, amount - fixed)
        return jnp.zeros((amount,), jnp.int32).at[ranking[jnp.where(places < fixed, places, shifted)]].set(jnp.asarray(sizes, jnp.int32))

    sizes = jnp.where(number % 4 == 0, named(crowded, number // 4), named(usual, number - number // 4 - 1))
    mixed = jax.random.permutation(jax.random.fold_in(own, 3), amount)
    donor, taker = mixed[0:amount // 2 * 2:2], mixed[1:amount // 2 * 2:2]
    room = jnp.minimum(sizes[donor] - 1, limit - sizes[taker]) // 2
    room = jnp.where((donor == ranking[0]) | (taker == ranking[0]) | (sizes[taker] == 0), 0, jnp.maximum(room, 0))
    shifted = jax.random.randint(jax.random.fold_in(own, 4), (amount // 2,), 0, 1 << 20) % (room + 1)
    sizes = sizes.at[donor].add(-shifted).at[taker].add(shifted)
    labels = jnp.searchsorted(jnp.cumsum(sizes), jnp.arange(rows * top), side="right").astype(jnp.int32)
    grid = labels.reshape(top, rows).T
    grid = grid[jax.random.permutation(jax.random.fold_in(own, 1), rows)]
    turn = jax.random.randint(jax.random.fold_in(own, 2), (rows, 1), 0, top)
    return jnp.take_along_axis(grid, (jnp.arange(top)[None, :] + turn) % top, axis=1)


def portions_of(number_of, total, reach, skew, full):
    weights = [(1 << 20) // math.isqrt(standing ** skew) + 1 for standing in range(1, number_of + 1)]
    largest = reach if full else min(reach, max(-(-total // number_of), total * weights[0] // sum(weights)))
    least = 1 if total - largest >= number_of - 1 else 0
    holding, rest = [largest] + [least] * (number_of - 1), total - largest - least * (number_of - 1)
    while rest > 0:
        movable = [i for i in range(1, number_of) if holding[i] < largest] or [i for i in range(1, number_of) if holding[i] < reach]
        whole, remaining = sum([weights[i] for i in movable]), rest
        for i in movable:
            more = min(reach - holding[i], max(1, remaining * weights[i] // whole), rest)
            holding[i] = holding[i] + more
            rest = rest - more
    return np.array(holding)


def normal_values(stream_key, shape, width, limit, shards=(), kind=jnp.bfloat16):
    drawn = width * jax.random.normal(stream_key, shape, jnp.float32)
    if shards:
        drawn = drawn * steps_of(stream_key, shape, shards, -0.22, 0.18)
    return jnp.clip(drawn, -limit, limit).astype(kind)


def setup_inputs(seed: int = 0) -> dict:
    seeds = jax.random.split(jax.random.key(seed), 10)
    queries = draw_queries(jax.random.fold_in(seeds[9], 71), 0)
    new_kv = draw_new_kv(jax.random.fold_in(seeds[9], 71), 0)
    prompt_key_value = normal_values(seeds[2], (2, PROMPT_TOTAL, PROMPT_LENGTH, KEY_HEADS * 2 * HEAD_SIZE), 2.0, 12.0, ((0, 2), (2, 16), (3, 8)))
    step_key_value = normal_values(seeds[3], (2, BEAM_TOTAL, STEP_LENGTH, KEY_HEADS * 2 * HEAD_SIZE), 2.0, 12.0, ((0, 2), (1, 16), (3, 8)))
    parent_dev_keys = jax.random.split(jax.random.fold_in(seeds[4], 1), BEAM_TOTAL // BEAM_DEV)
    parent_dev_turns = jax.random.permutation(jax.random.fold_in(seeds[4], 3), BEAM_TOTAL // BEAM_DEV)
    parent_dev = jax.vmap(lambda own, number: assign_block(jax.random.fold_in(seeds[4], 2), own, number, BEAM_DEV, HOLDERS, 1, MOST, 2))(parent_dev_keys, parent_dev_turns).reshape((BEAM_TOTAL, 1))
    parent_slot = with_ends(jax.random.randint(seeds[5], (BEAM_TOTAL,), 0, BEAM_DEV), jax.random.fold_in(seeds[5], 1), 0, BEAM_DEV - 1).astype(jnp.int32)
    cache_len = draw_cache_len(jax.random.fold_in(seeds[9], 71), 0)
    prompt_ids = with_ends(skewed_ids(seeds[7], (BEAM_TOTAL,), PROMPT_TOTAL, 2), jax.random.fold_in(seeds[7], 3), 0, PROMPT_TOTAL - 1).astype(jnp.int32)
    score_weights = normal_values(seeds[8], (2, QUERY_HEADS * HEAD_SIZE), (QUERY_HEADS * HEAD_SIZE) ** -0.5, 0.0625, ((0, 2), (1, 8)), jnp.float32)
    return {"queries": queries, "new_kv": new_kv, "prompt_key_value": prompt_key_value, "step_key_value": step_key_value, "parent_dev": parent_dev, "parent_slot": parent_slot, "cache_len": cache_len, "prompt_ids": prompt_ids, "score_weights": score_weights}


def reference(queries, new_kv, prompt_key_value, step_key_value, parent_dev, parent_slot, cache_len, prompt_ids, score_weights):
    queries_per_group = QUERY_HEADS // KEY_HEADS
    scale = 1.0 / math.sqrt(HEAD_SIZE)
    parent = (parent_dev[:, 0] * BEAM_DEV + parent_slot).astype(jnp.int32)
    key_count_total = PROMPT_LENGTH + STEP_LENGTH + NEW_TOKENS
    position = jnp.arange(key_count_total, dtype=jnp.int32)
    new_index = jnp.arange(NEW_TOKENS, dtype=jnp.int32)

    def per_beam(inputs):
        beam_index, prompt_no, parent_no, length = inputs
        query_rows = queries[:, beam_index].astype(jnp.float32).reshape(2, NEW_TOKENS, KEY_HEADS, queries_per_group, HEAD_SIZE)
        gathered_rows = jnp.concatenate([prompt_key_value[:, prompt_no], step_key_value[:, parent_no], new_kv[:, beam_index]], axis=1)
        gathered_rows = gathered_rows.astype(jnp.float32).reshape(2, key_count_total, KEY_HEADS, 2, HEAD_SIZE)
        key_matrix = gathered_rows[:, :, :, 0]
        value_matrix = gathered_rows[:, :, :, 1]
        scores = jnp.einsum('mrgjd,mkgd->mrgjk', query_rows, key_matrix, precision=lax.Precision.HIGHEST) * scale
        in_prompt = position < PROMPT_LENGTH
        in_step = (position >= PROMPT_LENGTH) & (position < PROMPT_LENGTH + STEP_LENGTH) & (position - PROMPT_LENGTH < length)
        in_new = (position >= PROMPT_LENGTH + STEP_LENGTH)[None, :] & ((position - PROMPT_LENGTH - STEP_LENGTH)[None, :] <= new_index[:, None])
        visible = (in_prompt | in_step)[None, :] | in_new
        visible = visible[None, :, None, None, :]
        scores = jnp.where(visible, scores, -1e+30)
        highest = lax.optimization_barrier(jnp.max(scores, axis=-1))
        weights = jnp.where(visible, jnp.exp(scores - highest[..., None]), 0.0)
        weight_sum = lax.optimization_barrier(jnp.sum(weights, axis=-1))
        summed = jnp.einsum('mrgjk,mkgd->mrgjd', weights, value_matrix, precision=lax.Precision.HIGHEST)
        result = summed / weight_sum[..., None]
        return result.reshape(2, NEW_TOKENS, QUERY_HEADS * HEAD_SIZE).astype(jnp.bfloat16)
    by_beam = lax.map(per_beam, (jnp.arange(BEAM_TOTAL, dtype=jnp.int32), prompt_ids, parent, cache_len))
    attended = jnp.transpose(by_beam, (1, 0, 2, 3))
    beam_score = jnp.einsum('mbrf,mf->b', attended.astype(jnp.float32), score_weights, precision=lax.Precision.HIGHEST) / NEW_TOKENS
    return (attended, beam_score)
```

```python
import functools
import math

import jax
import jax.numpy as jnp
from jax import lax
from jax.experimental import pallas as pl
from jax.experimental.pallas import tpu as pltpu
from jax.sharding import PartitionSpec as P

MESH = pl.DeviceIdType.MESH
F32, BF16, I32 = jnp.float32, jnp.bfloat16, jnp.int32

HEAD = 128
BEAMS = 64
ROWS = 32
CAP = 8
HOLD = 16
TILE = 8
TILES = BEAMS // TILE + 1
PLACES = TILES * TILE
TROWS = TILE * ROWS
SHARD = 256
NEWPAD = 16
SCALE = math.log2(math.e) / math.sqrt(HEAD)
LOW = -1e30
TAB = HOLD + PLACES


def iota(shape, axis):
    return lax.broadcasted_iota(I32, shape, axis)


def table_kernel(meta_ref, pid_ref, tab_ref):
    me = lax.axis_index("beam")
    upper = (iota((BEAMS, BEAMS), 0) < iota((BEAMS, BEAMS), 1)).astype(F32)
    pdev = meta_ref[0]
    slot = meta_ref[1].astype(F32)
    length = meta_ref[2].astype(F32)
    lane = iota((HOLD, 128), 1)
    head = jnp.zeros((HOLD, 128), F32)

    served = (pdev == me).astype(F32)
    rank = jnp.dot(served, upper, preferred_element_type=F32)
    mine = meta_ref[0, pl.ds(me, 1), :]
    ahead = (mine - me + HOLD) & (HOLD - 1)
    row16 = iota((HOLD, BEAMS), 0)
    own = (jnp.broadcast_to(ahead, (HOLD, BEAMS)) == row16).astype(F32)
    own_rank = jnp.dot(own, upper, preferred_element_type=F32)
    beam = iota((HOLD, BEAMS), 1).astype(F32)
    for k in range(CAP):
        pick = jnp.where(rank == k, served, 0.0)
        head = jnp.where(lane == k, jnp.sum(pick * slot, axis=1, keepdims=True), head)
        head = jnp.where(lane == CAP + k, jnp.sum(pick * length, axis=1, keepdims=True), head)
        pick = jnp.where(own_rank == k, own, 0.0)
        head = jnp.where(lane == 2 * CAP + k, jnp.sum(pick * beam, axis=1, keepdims=True), head)
    tab_ref[0:HOLD, :] = head.astype(I32)

    arrival = jnp.sum(own * (row16.astype(F32) * CAP + own_rank), axis=0, keepdims=True)
    first = (pid_ref[...] == 0).astype(F32)
    before = jnp.dot(jnp.broadcast_to(first, (8, BEAMS)), upper, preferred_element_type=F32)[0:1]
    count = jnp.sum(first, axis=1, keepdims=True).astype(I32)
    filled = (count + (TILE - 1)) & (-TILE)
    after = filled.astype(F32) + iota((1, BEAMS), 1).astype(F32) - before
    place = jnp.where(first > 0.5, before, after)

    lane = iota((PLACES, 128), 1)
    beam = iota((PLACES, BEAMS), 1).astype(F32)
    here = iota((PLACES, BEAMS), 0).astype(F32)
    at_place = (jnp.broadcast_to(place, (PLACES, BEAMS)) == here).astype(F32)
    holder = jnp.sum(at_place * beam, axis=1, keepdims=True)
    on_diag = (beam == here).astype(F32)
    arrival_col = jnp.sum(on_diag * arrival, axis=1, keepdims=True)
    place_col = jnp.sum(on_diag * place, axis=1, keepdims=True)
    tile_start = iota((PLACES, 128), 0) * TILE
    which = (tile_start >= filled).astype(F32)
    body = jnp.where(lane == 0, holder, 0.0)
    body = jnp.where(lane == 1, which, body)
    body = jnp.where(lane == 2, arrival_col, body)
    body = jnp.where(lane == 3, place_col, body)
    tab_ref[HOLD:TAB, :] = body.astype(I32)


OWN, XOWN, ANTI, XANTI = 0, 1, 14, 15
FWD = {1: 2, 2: 6, 3: 10}
BWD = {1: 3, 2: 7, 3: 11}
XFWD = {1: 4, 2: 8, 3: 12}
XBWD = {1: 5, 2: 9, 3: 13}


def dot_nt(a, b):
    return lax.dot_general(a, b, (((1,), (1,)), ((), ())), preferred_element_type=F32)


def dot_nn(a, b):
    return lax.dot_general(a, b, (((1,), (0,)), ((), ())), preferred_element_type=F32)


def main_kernel(
    groups, lanes_tp, tab, q_ref, kvn_ref, w_ref, prompt_hbm, pages_hbm,
    out_ref, score_ref,
    pages, kv0, kv1, kv2, kv3, send, recv, ret_out, ret_in, stat_out, stat_in,
    qt, kvt, acc, high, part, share, shares,
    q_ss, q_rs, r_ss, r_rs, s_ss, s_rs, f_ss, f_rs, b_ss, b_rs, x_ss, x_rs, c_ss, c_rs, l_sem,
):
    me = lax.axis_index("beam")
    grp = lax.axis_index("grp")
    tp = lax.axis_index("tp")
    group = grp * lanes_tp + tp
    up = lax.rem(me + 2, HOLD)
    down = lax.rem(me + HOLD - 2, HOLD)
    side = me + 1 - 2 * lax.rem(me, 2)

    held = (kv0, kv1, kv2, kv3)

    def shard_at(slot):
        return held[slot // 4].at[slot % 4]

    load_prompt = pltpu.make_async_copy(prompt_hbm, shard_at(OWN), l_sem.at[0])
    load_pages = pltpu.make_async_copy(pages_hbm, pages, l_sem.at[1])
    load_prompt.start()
    load_pages.start()

    barrier = pltpu.get_barrier_semaphore()

    def greet_beam(o, _):
        pl.semaphore_signal(barrier, inc=1, device_id={"beam": lax.rem(me + o, HOLD)}, device_id_type=MESH)
        return 0

    lax.fori_loop(1, HOLD, greet_beam, 0)

    def group_peer(o):
        peer = lax.rem(group + o, groups)
        return {"grp": lax.div(peer, lanes_tp), "tp": lax.rem(peer, lanes_tp)}

    if groups > 1:
        def greet_group(o, _):
            pl.semaphore_signal(barrier, inc=1, device_id=group_peer(o), device_id_type=MESH)
            return 0

        lax.fori_loop(1, groups, greet_group, 0)

    def span(o):
        return pl.ds(o * CAP, CAP)

    def pack(o, into):
        for k in range(CAP):
            into[o * CAP + k] = q_ref[tab[o, 2 * CAP + k]]

    pack(0, recv)
    pl.semaphore_wait(barrier, HOLD - 1 + groups - 1)

    def query_copy(o):
        return pltpu.make_async_remote_copy(
            src_ref=send.at[span(o)], dst_ref=recv.at[span(o)], send_sem=q_ss.at[o], recv_sem=q_rs.at[o],
            device_id={"beam": lax.rem(me + o, HOLD)}, device_id_type=MESH)

    def send_query(o, _):
        pack(o, send)
        query_copy(o).start()
        return 0

    lax.fori_loop(1, HOLD, send_query, 0)

    def shard_copy(src, dst, to, ss, rs, half=None):
        a, b = shard_at(src), shard_at(dst)
        if half is not None:
            a, b = a.at[half], b.at[half]
        return pltpu.make_async_remote_copy(
            src_ref=a, dst_ref=b, send_sem=ss, recv_sem=rs, device_id={"beam": to}, device_id_type=MESH)

    def fwd_copy(s):
        src = OWN if s == 1 else FWD[s - 1]
        if s == 4:
            return shard_copy(src, ANTI, up, f_ss.at[s], f_rs.at[s], 0)
        return shard_copy(src, FWD[s], up, f_ss.at[s], f_rs.at[s])

    def bwd_copy(s):
        src = OWN if s == 1 else BWD[s - 1]
        if s == 4:
            return shard_copy(src, ANTI, down, b_ss.at[s], b_rs.at[s], 1)
        return shard_copy(src, BWD[s], down, b_ss.at[s], b_rs.at[s])

    x_plan = [(OWN, XOWN)]
    for s in (1, 2, 3):
        x_plan += [(FWD[s], XFWD[s]), (BWD[s], XBWD[s])]
    x_plan += [(ANTI, XANTI)]

    def x_copy(i):
        src, dst = x_plan[i]
        return shard_copy(src, dst, side, x_ss.at[i], x_rs.at[i])

    load_prompt.wait()
    fwd_copy(1).start()
    bwd_copy(1).start()
    x_copy(0).start()

    def ring_step(s):
        fwd_copy(s).wait_recv()
        if s < 4:
            fwd_copy(s + 1).start()
            x_copy(2 * s - 1).start()
        bwd_copy(s).wait_recv()
        if s < 4:
            bwd_copy(s + 1).start()
            x_copy(2 * s).start()
        else:
            x_copy(7).start()

    def fill_tile(t, _):
        for i in range(TILE):
            b = tab[HOLD + t * TILE + i, 0]
            qt[t * TILE + i] = q_ref[b]
            kvt[t * TILE + i] = kvn_ref[b]
        return 0

    lax.fori_loop(0, TILES, fill_tile, 0)

    def with_ones(values):
        return jnp.concatenate([values, jnp.ones(values.shape, BF16)], axis=1)

    diag = (iota((TROWS, 128), 0) & 127) == iota((TROWS, 128), 1)
    column = iota((ROWS, 128), 1)

    def step_part(o, into_out, into_stat):
        c = lax.rem(me - o + HOLD, HOLD)
        blocks = []
        values = []
        for j in range(CAP // 2):
            k0, k1 = 2 * j, 2 * j + 1
            page0, page1 = pages[tab[c, k0]], pages[tab[c, k1]]
            keys = jnp.concatenate([page0[:, :HEAD], page1[:, :HEAD]], axis=0)
            values.append(with_ones(jnp.concatenate([page0[:, HEAD:], page1[:, HEAD:]], axis=0)))
            queries = recv[pl.ds(o * CAP + k0, 2)].reshape(2 * ROWS, HEAD)
            s = dot_nt(queries, keys)
            blocks.append(jnp.where(column < tab[c, CAP + k0], s[:ROWS, :128] * SCALE, LOW))
            blocks.append(jnp.where(column < tab[c, CAP + k1], s[ROWS:, 128:] * SCALE, LOW))
        s = jnp.concatenate(blocks, axis=0)
        top = jnp.max(s, axis=1, keepdims=True)
        p = jnp.exp2(s - top).astype(BF16)
        zero = jnp.zeros((ROWS, 128), BF16)
        sums = []
        for j in range(CAP // 2):
            p0, p1 = p[2 * j * ROWS:(2 * j + 1) * ROWS], p[(2 * j + 1) * ROWS:(2 * j + 2) * ROWS]
            wide = jnp.concatenate(
                [jnp.concatenate([p0, zero], axis=1), jnp.concatenate([zero, p1], axis=1)], axis=0)
            sums.append(dot_nn(wide, values[j]))
        sums = jnp.concatenate(sums, axis=0)
        total = sums[:, HEAD:]
        into_out[span(o)] = (sums[:, :HEAD] / total).astype(BF16).reshape(CAP, ROWS, HEAD)
        level = top + jnp.log2(total)
        flat = jnp.sum(jnp.where(diag, level, 0.0).reshape(2, 128, 128), axis=1)
        into_stat[o] = jnp.concatenate([flat, jnp.zeros((6, 128), F32)], axis=0)

    def back_copy(o):
        to = {"beam": lax.rem(me - o + HOLD, HOLD)}
        return (
            pltpu.make_async_remote_copy(
                src_ref=ret_out.at[span(o)], dst_ref=ret_in.at[span(o)], send_sem=r_ss.at[o],
                recv_sem=r_rs.at[o], device_id=to, device_id_type=MESH),
            pltpu.make_async_remote_copy(
                src_ref=stat_out.at[o], dst_ref=stat_in.at[o], send_sem=s_ss.at[o],
                recv_sem=s_rs.at[o], device_id=to, device_id_type=MESH),
        )

    def serve(o, _):
        query_copy(o).wait_recv()
        step_part(o, ret_out, stat_out)
        for copy in back_copy(o):
            copy.start()
        return 0

    load_pages.wait()
    step_part(0, ret_in, stat_in)

    def new_part(t, _):
        q = qt[pl.ds(t * TILE, TILE)].reshape(TROWS, HEAD)
        kv = kvt[pl.ds(t * TILE, TILE)].reshape(TILE * NEWPAD, 2 * HEAD)
        row, col = iota((TROWS, TILE * NEWPAD), 0), iota((TROWS, TILE * NEWPAD), 1)
        seen = ((row >> 5) == (col >> 4)) & ((col & 15) <= ((row >> 3) & 3))
        s = jnp.where(seen, dot_nt(q, kv[:, :HEAD]) * SCALE, LOW)
        top = jnp.max(s, axis=1, keepdims=True)
        p = jnp.exp2(s - top).astype(BF16)
        acc[pl.ds(t * TILE, TILE)] = dot_nn(p, with_ones(kv[:, HEAD:])).reshape(TILE, ROWS, 2 * HEAD)
        high[pl.ds(t * TILE, TILE)] = jnp.broadcast_to(top, (TROWS, 128)).reshape(TILE, ROWS, 128)
        return 0

    lax.fori_loop(0, TILES, new_part, 0)

    lax.fori_loop(1, 5, serve, 0)
    ring_step(1)
    lax.fori_loop(5, 9, serve, 0)
    ring_step(2)
    lax.fori_loop(9, 13, serve, 0)
    ring_step(3)
    lax.fori_loop(13, 16, serve, 0)

    def prompt_part(number):
        def one(t, _):
            own = tab[HOLD + t, 1]
            q = qt[pl.ds(t * TILE, TILE)].reshape(TROWS, HEAD)
            kv = held[number][:, own].reshape(4 * SHARD, 2 * HEAD)
            s = dot_nt(q, kv[:, :HEAD]) * SCALE
            old = high[pl.ds(t * TILE, TILE)].reshape(TROWS, 128)
            top = jnp.maximum(old, jnp.max(s, axis=1, keepdims=True))
            p = jnp.exp2(s - top[:, :1]).astype(BF16)
            fade = jnp.exp2(old - top)
            add = dot_nn(p, with_ones(kv[:, HEAD:]))
            was = acc[pl.ds(t * TILE, TILE)].reshape(TROWS, 2 * HEAD)
            new = was * jnp.concatenate([fade, fade], axis=1) + add
            acc[pl.ds(t * TILE, TILE)] = new.reshape(TILE, ROWS, 2 * HEAD)
            high[pl.ds(t * TILE, TILE)] = top.reshape(TILE, ROWS, 128)
            return 0

        lax.fori_loop(0, TILES, one, 0)

    x_copy(0).wait_recv()
    prompt_part(0)
    ring_step(4)
    for i in (1, 2):
        x_copy(i).wait_recv()
    prompt_part(1)
    for i in (3, 4):
        x_copy(i).wait_recv()
    prompt_part(2)
    for i in (5, 6, 7):
        x_copy(i).wait_recv()
    prompt_part(3)

    def await_back(o, _):
        for copy in back_copy(o):
            copy.wait_recv()
        return 0

    lax.fori_loop(1, HOLD, await_back, 0)

    lane_of = iota((ROWS, 128), 1) - iota((ROWS, 128), 0)

    def finish(i, _):
        for u in range(4):
            b = i * 4 + u
            a = tab[HOLD + b, 2]
            place = tab[HOLD + b, 3]
            line = stat_in[a >> 3, pl.ds((a >> 2) & 1, 1), :]
            level = jnp.sum(jnp.where(lane_of == (a & 3) * ROWS, line, 0.0), axis=1, keepdims=True)
            old = high[place]
            top = jnp.maximum(old, level)
            mine, theirs = jnp.exp2(old - top), jnp.exp2(level - top)
            sums = acc[place]
            whole = sums[:, :HEAD] * mine + ret_in[a].astype(F32) * theirs
            result = (whole / (sums[:, HEAD:] * mine + theirs)).astype(BF16)
            out_ref[b] = result
            part[pl.ds(b, 1), :] = jnp.sum(result.astype(F32) * w_ref[...], axis=0, keepdims=True)
        return 0

    lax.fori_loop(0, BEAMS // 4, finish, 0)

    score = jnp.sum(part[...], axis=1, keepdims=True)
    spot = iota((BEAMS, 128), 0) == iota((BEAMS, 128), 1)
    line = jnp.sum(jnp.where(spot, score, 0.0), axis=0, keepdims=True) * 0.25
    share[...] = jnp.broadcast_to(line, (8, 128))
    if groups > 1:
        def share_copy(o):
            return pltpu.make_async_remote_copy(
                src_ref=share, dst_ref=shares.at[group], send_sem=c_ss.at[o], recv_sem=c_rs.at[o],
                device_id=group_peer(o), device_id_type=MESH)

        def send_share(o, _):
            share_copy(o).start()
            return 0

        lax.fori_loop(1, groups, send_share, 0)
        shares[group] = share[...]

        def await_share(o, _):
            share_copy(o).wait()
            return 0

        lax.fori_loop(1, groups, await_share, 0)
        score_ref[...] = jnp.sum(shares[...], axis=0)
    else:
        score_ref[...] = share[...]

    def await_sends(o, _):
        query_copy(o).wait_send()
        for copy in back_copy(o):
            copy.wait_send()
        return 0

    lax.fori_loop(1, HOLD, await_sends, 0)
    for s in (1, 2, 3, 4):
        fwd_copy(s).wait_send()
        bwd_copy(s).wait_send()
    for i in range(8):
        x_copy(i).wait_send()


def on_device(queries, new_kv, prompt_key_value, step_key_value, parent_dev, parent_slot, cache_len, prompt_ids, score_weights):
    lanes_tp = lax.axis_size("tp")
    groups = lax.axis_size("grp") * lanes_tp
    meta = jnp.stack([parent_dev[:, 0], parent_slot, cache_len]).reshape(3, HOLD, BEAMS)
    vmem = pl.BlockSpec(memory_space=pltpu.VMEM)
    smem = pl.BlockSpec(memory_space=pltpu.SMEM)
    anywhere = pl.BlockSpec(memory_space=pl.ANY)
    table = pl.pallas_call(
        table_kernel,
        out_shape=jax.ShapeDtypeStruct((TAB, 128), I32),
        in_specs=[vmem, vmem],
        out_specs=vmem,
    )(meta, prompt_ids.reshape(1, BEAMS))
    q = queries.reshape(BEAMS, ROWS, HEAD)
    kvn = jnp.pad(new_kv[0], ((0, 0), (0, NEWPAD - new_kv.shape[2]), (0, 0)))
    weights = jnp.tile(score_weights.reshape(8, HEAD), (4, 1))
    dma = pltpu.SemaphoreType.DMA
    attended, score = pl.pallas_call(
        functools.partial(main_kernel, groups, lanes_tp),
        out_shape=(
            jax.ShapeDtypeStruct((BEAMS, ROWS, HEAD), BF16),
            jax.ShapeDtypeStruct((8, 128), F32),
        ),
        in_specs=[smem, vmem, vmem, vmem, anywhere, anywhere],
        out_specs=(vmem, vmem),
        scratch_shapes=[
            pltpu.VMEM((BEAMS, 128, 2 * HEAD), BF16),
        ] + [pltpu.VMEM((4, 2, SHARD, 2 * HEAD), BF16)] * 4 + [
            pltpu.VMEM((HOLD * CAP, ROWS, HEAD), BF16),
            pltpu.VMEM((HOLD * CAP, ROWS, HEAD), BF16),
            pltpu.VMEM((HOLD * CAP, ROWS, HEAD), BF16),
            pltpu.VMEM((HOLD * CAP, ROWS, HEAD), BF16),
            pltpu.VMEM((HOLD, 8, 128), F32),
            pltpu.VMEM((HOLD, 8, 128), F32),
            pltpu.VMEM((PLACES, ROWS, HEAD), BF16),
            pltpu.VMEM((PLACES, NEWPAD, 2 * HEAD), BF16),
            pltpu.VMEM((PLACES, ROWS, 2 * HEAD), F32),
            pltpu.VMEM((PLACES, ROWS, 128), F32),
            pltpu.VMEM((BEAMS, 128), F32),
            pltpu.VMEM((8, 128), F32),
            pltpu.VMEM((max(groups, 1), 8, 128), F32),
        ] + [dma((HOLD,))] * 6 + [dma((5,))] * 4 + [dma((8,))] * 2 + [dma((max(groups, 1),))] * 2 + [dma((2,))],
        compiler_params=pltpu.CompilerParams(
            collective_id=0, has_side_effects=True, vmem_limit_bytes=48 * 1024 * 1024),
    )(table, q, kvn, weights, prompt_key_value[0], step_key_value[0])
    return attended.reshape(1, BEAMS, 4, 8 * HEAD), score[0, :BEAMS]


def solution(mesh):
    in_specs = (
        P("grp", "beam", None, "tp"),
        P("grp", "beam", None, "tp"),
        P("grp", None, "beam", "tp"),
        P("grp", "beam", None, "tp"),
        P(),
        P(),
        P(),
        P("beam"),
        P("grp", "tp"),
    )
    out_specs = (P("grp", "beam", None, "tp"), P("beam"))
    return jax.shard_map(on_device, mesh=mesh, in_specs=in_specs, out_specs=out_specs, check_vma=False)
```

```python
import functools
import math

import jax
import jax.numpy as jnp
from jax import lax
from jax.experimental import pallas as pl
from jax.experimental.pallas import tpu as pltpu
from jax.sharding import PartitionSpec as P

MESH = pl.DeviceIdType.MESH
F32, BF16, I32 = jnp.float32, jnp.bfloat16, jnp.int32

HEAD = 128
BEAMS = 64
ROWS = 32
CAP = 8
HOLD = 16
TILE = 8
TILES = BEAMS // TILE + 1
PLACES = TILES * TILE
TROWS = TILE * ROWS
SHARD = 256
NEWPAD = 16
SCALE = math.log2(math.e) / math.sqrt(HEAD)
LOW = -1e30
VMEM_LIMIT = 61 * 1024 * 1024
TAB = 32
INV, PLACED, PROMPT, ARRIVAL, PLACE = 8, 24, 25, 26, 27


def iota(shape, axis):
    return lax.broadcasted_iota(I32, shape, axis)


def table_kernel(pdev_ref, slot_ref, length_ref, pid_ref, tab_ref):
    me = lax.axis_index("beam")
    z, x = lax.div(me, 2), lax.rem(me, 2)
    pdev = pdev_ref[...]
    code = (slot_ref[...] * 256 + length_ref[...]).astype(F32)

    a, b = iota((128, 128), 0), iota((128, 128), 1)
    upper = ((a < b) & ((a >> 6) == (b >> 6))).astype(F32)
    served = (pdev == me).astype(F32)
    rank = jnp.dot(served, upper, preferred_element_type=F32)
    lane = iota((8, 128), 1)
    head = jnp.zeros((8, 128), F32)
    for k in range(CAP):
        pick = jnp.where(rank == k, served, 0.0) * code
        for h in range(2):
            found = jnp.sum(jnp.where((lane >> 6) == h, pick, 0.0), axis=1, keepdims=True)
            head = jnp.where(lane == h * CAP + k, found, head)
    tab_ref[0:8, :] = head.astype(I32)

    upper = upper[:BEAMS, :BEAMS]
    pair = pdev_ref[pl.ds(z, 1), :]
    mine = jnp.where(x == 1, pair[:, BEAMS:], pair[:, :BEAMS])
    ahead = (((mine >> 1) - z) & 7) * 2 + ((mine - x) & 1)
    offset = iota((HOLD, BEAMS), 0)
    beam = iota((HOLD, BEAMS), 1).astype(F32)
    own = (jnp.broadcast_to(ahead, (HOLD, BEAMS)) == offset).astype(F32)
    own_rank = jnp.dot(own, upper, preferred_element_type=F32)
    lane = iota((HOLD, 128), 1)
    body = jnp.zeros((HOLD, 128), F32)
    for k in range(CAP):
        found = jnp.sum(jnp.where(own_rank == k, own, 0.0) * beam, axis=1, keepdims=True)
        body = jnp.where(lane == k, found, body)
    tab_ref[8:8 + HOLD, :] = body.astype(I32)

    arrival = jnp.sum(own * (offset.astype(F32) * CAP + own_rank), axis=0, keepdims=True)
    first = (pid_ref[...] == 0).astype(F32)
    before = jnp.dot(jnp.broadcast_to(first, (8, BEAMS)), upper, preferred_element_type=F32)[0:1]
    count = jnp.sum(first, axis=1, keepdims=True).astype(I32)
    filled = (count + (TILE - 1)) & (-TILE)
    after = filled.astype(F32) + iota((1, BEAMS), 1).astype(F32) - before
    place = jnp.where(first > 0.5, before, after)
    diagonal = iota((BEAMS, BEAMS), 0) == iota((BEAMS, BEAMS), 1)
    column = jnp.sum(jnp.where(diagonal, place, 0.0), axis=1, keepdims=True)
    there = column == iota((BEAMS, 128), 1).astype(F32)
    holder = jnp.sum(jnp.where(there, iota((BEAMS, 128), 0).astype(F32), 0.0), axis=0, keepdims=True)
    which = (iota((1, 128), 1) * TILE >= filled).astype(F32)
    rest = jnp.zeros((1, 128 - BEAMS), F32)
    tail = jnp.concatenate([
        holder, which, jnp.concatenate([arrival, rest], axis=1), jnp.concatenate([place, rest], axis=1),
        jnp.zeros((4, 128), F32)], axis=0)
    tab_ref[24:32, :] = tail.astype(I32)


OWN, XOWN, ANTI, XANTI = 0, 1, 14, 15
FWD = {1: 2, 2: 6, 3: 10}
BWD = {1: 3, 2: 7, 3: 11}
XFWD = {1: 4, 2: 8, 3: 12}
XBWD = {1: 5, 2: 9, 3: 13}


def dot_nt(a, b):
    return lax.dot_general(a, b, (((1,), (1,)), ((), ())), preferred_element_type=F32)


def dot_nn(a, b):
    return lax.dot_general(a, b, (((1,), (0,)), ((), ())), preferred_element_type=F32)


def main_kernel(
    groups, lanes_tp, tab_any, q_ref, kvn_ref, w_ref, prompt_hbm, pages_hbm,
    out_ref, score_ref,
    tab, pages, kv0, kv1, kv2, kv3, send, recv, ret_out, ret_in, stat_out, stat_in,
    qt, kvt, acc, high, part, share, shares,
    q_ss, q_rs, r_ss, r_rs, s_ss, s_rs, f_ss, f_rs, b_ss, b_rs, x_ss, x_rs, c_ss, c_rs, l_sem,
):
    me = lax.axis_index("beam")
    grp = lax.axis_index("grp")
    tp = lax.axis_index("tp")
    group = grp * lanes_tp + tp
    z, x = lax.div(me, 2), lax.rem(me, 2)

    def at(dz, dx):
        return lax.rem(z + dz + 8, 8) * 2 + lax.rem(x + dx, 2)

    def target(o):
        return at(lax.div(o, 2), lax.rem(o, 2))

    def origin(o):
        return at(-lax.div(o, 2), lax.rem(o, 2))

    def near(i):
        g, r = lax.div(i - 1, 4), lax.rem(i - 1, 4)
        return (g + 1 + lax.div(r, 2) * (6 - 2 * g)) * 2 + lax.rem(r, 2)

    up, down, side = at(1, 0), at(-1, 0), at(0, 1)

    held = (kv0, kv1, kv2, kv3)

    def shard_at(slot):
        return held[slot // 4].at[slot % 4]

    load_prompt = pltpu.make_async_copy(prompt_hbm, shard_at(OWN), l_sem.at[0])
    load_pages = pltpu.make_async_copy(pages_hbm, pages, l_sem.at[1])
    load_table = pltpu.make_async_copy(tab_any, tab, l_sem.at[2])
    load_table.start()
    load_prompt.start()
    load_pages.start()

    barrier = pltpu.get_barrier_semaphore()

    def greet_beam(o, _):
        pl.semaphore_signal(barrier, inc=1, device_id={"beam": lax.rem(me + o, HOLD)}, device_id_type=MESH)
        return 0

    lax.fori_loop(1, HOLD, greet_beam, 0)

    def group_peer(o):
        peer = lax.rem(group + o, groups)
        return {"grp": lax.div(peer, lanes_tp), "tp": lax.rem(peer, lanes_tp)}

    if groups > 1:
        def greet_group(o, _):
            pl.semaphore_signal(barrier, inc=1, device_id=group_peer(o), device_id_type=MESH)
            return 0

        lax.fori_loop(1, groups, greet_group, 0)

    def span(o):
        return pl.ds(o * CAP, CAP)

    load_table.wait()

    def pack(o, into):
        for k in range(CAP):
            into[o * CAP + k] = q_ref[tab[INV + o, k]]

    def pack_for(o, _):
        pack(o, send)
        return 0

    pack(0, recv)
    lax.fori_loop(1, HOLD, pack_for, 0)
    load_prompt.wait()
    pl.semaphore_wait(barrier, HOLD - 1 + groups - 1)

    def query_copy(o):
        return pltpu.make_async_remote_copy(
            src_ref=send.at[span(o)], dst_ref=recv.at[span(o)], send_sem=q_ss.at[o], recv_sem=q_rs.at[o],
            device_id={"beam": target(o)}, device_id_type=MESH)

    def send_near(i, _):
        query_copy(near(i)).start()
        return 0

    def shard_copy(src, dst, to, ss, rs, half=None):
        a, b = shard_at(src), shard_at(dst)
        if half is not None:
            a, b = a.at[half], b.at[half]
        return pltpu.make_async_remote_copy(
            src_ref=a, dst_ref=b, send_sem=ss, recv_sem=rs, device_id={"beam": to}, device_id_type=MESH)

    def fwd_copy(s):
        src = OWN if s == 1 else FWD[s - 1]
        if s == 4:
            return shard_copy(src, ANTI, up, f_ss.at[s], f_rs.at[s], 0)
        return shard_copy(src, FWD[s], up, f_ss.at[s], f_rs.at[s])

    def bwd_copy(s):
        src = OWN if s == 1 else BWD[s - 1]
        if s == 4:
            return shard_copy(src, ANTI, down, b_ss.at[s], b_rs.at[s], 1)
        return shard_copy(src, BWD[s], down, b_ss.at[s], b_rs.at[s])

    x_plan = [(OWN, XOWN)]
    for s in (1, 2, 3):
        x_plan += [(FWD[s], XFWD[s]), (BWD[s], XBWD[s])]
    x_plan += [(ANTI, XANTI)]

    def x_copy(i):
        src, dst = x_plan[i]
        return shard_copy(src, dst, side, x_ss.at[i], x_rs.at[i])

    fwd_copy(1).start()
    bwd_copy(1).start()
    x_copy(0).start()
    query_copy(1).start()
    lax.fori_loop(1, 5, send_near, 0)

    def ring_step(s):
        fwd_copy(s).wait_recv()
        if s < 4:
            fwd_copy(s + 1).start()
            x_copy(2 * s - 1).start()
        bwd_copy(s).wait_recv()
        if s < 4:
            bwd_copy(s + 1).start()
            x_copy(2 * s).start()
        else:
            x_copy(7).start()

    def fill_tile(t, _):
        for i in range(TILE):
            b = tab[PLACED, t * TILE + i]
            qt[t * TILE + i] = q_ref[b]
            kvt[t * TILE + i] = kvn_ref[b]
        return 0

    lax.fori_loop(0, TILES, fill_tile, 0)

    def with_ones(values):
        return jnp.concatenate([values, jnp.ones(values.shape, BF16)], axis=1)

    diag = (iota((TROWS, 128), 0) & 127) == iota((TROWS, 128), 1)
    column = iota((ROWS, 128), 1)

    def step_part(o, into_out, into_stat):
        c = origin(o)
        row, lane = lax.div(c, 2), lax.rem(c, 2) * CAP
        blocks = []
        values = []
        for j in range(CAP // 2):
            k0 = 2 * j
            code0, code1 = tab[row, lane + k0], tab[row, lane + k0 + 1]
            page0, page1 = pages[code0 >> 8], pages[code1 >> 8]
            keys = jnp.concatenate([page0[:, :HEAD], page1[:, :HEAD]], axis=0)
            values.append(with_ones(jnp.concatenate([page0[:, HEAD:], page1[:, HEAD:]], axis=0)))
            queries = recv[pl.ds(o * CAP + k0, 2)].reshape(2 * ROWS, HEAD)
            s = dot_nt(queries, keys)
            blocks.append(jnp.where(column < (code0 & 255), s[:ROWS, :128] * SCALE, LOW))
            blocks.append(jnp.where(column < (code1 & 255), s[ROWS:, 128:] * SCALE, LOW))
        s = jnp.concatenate(blocks, axis=0)
        top = jnp.max(s, axis=1, keepdims=True)
        p = jnp.exp2(s - top).astype(BF16)
        zero = jnp.zeros((ROWS, 128), BF16)
        sums = []
        for j in range(CAP // 2):
            p0, p1 = p[2 * j * ROWS:(2 * j + 1) * ROWS], p[(2 * j + 1) * ROWS:(2 * j + 2) * ROWS]
            wide = jnp.concatenate(
                [jnp.concatenate([p0, zero], axis=1), jnp.concatenate([zero, p1], axis=1)], axis=0)
            sums.append(dot_nn(wide, values[j]))
        sums = jnp.concatenate(sums, axis=0)
        total = sums[:, HEAD:]
        into_out[span(o)] = (sums[:, :HEAD] / total).astype(BF16).reshape(CAP, ROWS, HEAD)
        level = top + jnp.log2(total)
        flat = jnp.sum(jnp.where(diag, level, 0.0).reshape(2, 128, 128), axis=1)
        into_stat[o] = jnp.concatenate([flat, jnp.zeros((6, 128), F32)], axis=0)

    def back_copy(o):
        to = {"beam": origin(o)}
        return (
            pltpu.make_async_remote_copy(
                src_ref=ret_out.at[span(o)], dst_ref=ret_in.at[span(o)], send_sem=r_ss.at[o],
                recv_sem=r_rs.at[o], device_id=to, device_id_type=MESH),
            pltpu.make_async_remote_copy(
                src_ref=stat_out.at[o], dst_ref=stat_in.at[o], send_sem=s_ss.at[o],
                recv_sem=s_rs.at[o], device_id=to, device_id_type=MESH),
        )

    def serve(i, _):
        o = near(i)
        query_copy(o).wait_recv()
        step_part(o, ret_out, stat_out)
        for copy in back_copy(o):
            copy.start()
        return 0

    def new_part(t, _):
        q = qt[pl.ds(t * TILE, TILE)].reshape(TROWS, HEAD)
        kv = kvt[pl.ds(t * TILE, TILE)].reshape(TILE * NEWPAD, 2 * HEAD)
        row, col = iota((TROWS, TILE * NEWPAD), 0), iota((TROWS, TILE * NEWPAD), 1)
        seen = ((row >> 5) == (col >> 4)) & ((col & 15) <= ((row >> 3) & 3))
        s = jnp.where(seen, dot_nt(q, kv[:, :HEAD]) * SCALE, LOW)
        top = jnp.max(s, axis=1, keepdims=True)
        p = jnp.exp2(s - top).astype(BF16)
        acc[pl.ds(t * TILE, TILE)] = dot_nn(p, with_ones(kv[:, HEAD:])).reshape(TILE, ROWS, 2 * HEAD)
        high[pl.ds(t * TILE, TILE)] = jnp.broadcast_to(top, (TROWS, 128)).reshape(TILE, ROWS, 128)
        return 0

    def prompt_part(number):
        def one(t):
            own = tab[PROMPT, t]
            q = qt[pl.ds(t * TILE, TILE)].reshape(TROWS, HEAD)
            kv = held[number][:, own].reshape(4 * SHARD, 2 * HEAD)
            s = dot_nt(q, kv[:, :HEAD])
            cols = [s[:, i * 128:(i + 1) * 128] for i in range(4 * SHARD // 128)]
            top = functools.reduce(jnp.maximum, cols)
            old = high[pl.ds(t * TILE, TILE)].reshape(TROWS, 128)
            top = jnp.maximum(old, jnp.max(top, axis=1, keepdims=True) * SCALE)
            p = jnp.concatenate([jnp.exp2(col * SCALE - top).astype(BF16) for col in cols], axis=1)
            fade = jnp.exp2(old - top)
            add = dot_nn(p, with_ones(kv[:, HEAD:]))
            was = acc[pl.ds(t * TILE, TILE)].reshape(TROWS, 2 * HEAD)
            new = was * jnp.concatenate([fade, fade], axis=1) + add
            acc[pl.ds(t * TILE, TILE)] = new.reshape(TILE, ROWS, 2 * HEAD)
            high[pl.ds(t * TILE, TILE)] = top.reshape(TILE, ROWS, 128)

        def some(i, _):
            for u in range(3):
                one(i * 3 + u)
            return 0

        lax.fori_loop(0, TILES // 3, some, 0)

    def query_first(_):
        query_copy(1).wait_recv()
        step_part(1, ret_out, stat_out)
        for copy in back_copy(1):
            copy.start()

    load_pages.wait()
    step_part(0, ret_in, stat_in)
    lax.fori_loop(0, TILES, new_part, 0)
    ring_step(1)
    lax.fori_loop(5, 9, send_near, 0)
    ring_step(2)
    lax.fori_loop(9, 15, send_near, 0)
    query_first(0)
    lax.fori_loop(1, 5, serve, 0)
    ring_step(3)
    x_copy(0).wait_recv()
    prompt_part(0)
    lax.fori_loop(5, 9, serve, 0)
    ring_step(4)
    lax.fori_loop(9, 15, serve, 0)
    for i in (1, 2):
        x_copy(i).wait_recv()
    prompt_part(1)
    for i in (3, 4):
        x_copy(i).wait_recv()
    prompt_part(2)
    for i in (5, 6, 7):
        x_copy(i).wait_recv()
    prompt_part(3)

    def await_back(o, _):
        for copy in back_copy(o):
            copy.wait_recv()
        return 0

    lax.fori_loop(1, HOLD, await_back, 0)

    lane_of = iota((ROWS, 128), 1) - iota((ROWS, 128), 0)

    weights = jnp.concatenate([w_ref[...]] * 4, axis=0)

    def finish(i, _):
        for u in range(4):
            b = i * 4 + u
            a = tab[ARRIVAL, b]
            place = tab[PLACE, b]
            line = stat_in[a >> 3, pl.ds((a >> 2) & 1, 1), :]
            level = jnp.sum(jnp.where(lane_of == (a & 3) * ROWS, line, 0.0), axis=1, keepdims=True)
            old = high[place]
            top = jnp.maximum(old, level)
            mine, theirs = jnp.exp2(old - top), jnp.exp2(level - top)
            sums = acc[place]
            whole = sums[:, :HEAD] * mine + ret_in[a].astype(F32) * theirs
            result = (whole / (sums[:, HEAD:] * mine + theirs)).astype(BF16)
            out_ref[b] = result
            part[pl.ds(b, 1), :] = jnp.sum(result.astype(F32) * weights, axis=0, keepdims=True)
        return 0

    lax.fori_loop(0, BEAMS // 4, finish, 0)

    score = jnp.sum(part[...], axis=1, keepdims=True)
    spot = iota((BEAMS, 128), 0) == iota((BEAMS, 128), 1)
    line = jnp.sum(jnp.where(spot, score, 0.0), axis=0, keepdims=True) * 0.25
    share[...] = jnp.broadcast_to(line, (8, 128))
    if groups > 1:
        def share_copy(o):
            return pltpu.make_async_remote_copy(
                src_ref=share, dst_ref=shares.at[group], send_sem=c_ss.at[o], recv_sem=c_rs.at[o],
                device_id=group_peer(o), device_id_type=MESH)

        def send_share(o, _):
            share_copy(o).start()
            return 0

        lax.fori_loop(1, groups, send_share, 0)
        shares[group] = share[...]

        def await_share(o, _):
            share_copy(o).wait()
            return 0

        lax.fori_loop(1, groups, await_share, 0)
        score_ref[...] = jnp.sum(shares[...], axis=0)
    else:
        score_ref[...] = share[...]

    def await_sends(o, _):
        query_copy(o).wait_send()
        for copy in back_copy(o):
            copy.wait_send()
        return 0

    lax.fori_loop(1, HOLD, await_sends, 0)
    for s in (1, 2, 3, 4):
        fwd_copy(s).wait_send()
        bwd_copy(s).wait_send()
    for i in range(8):
        x_copy(i).wait_send()


def on_device(queries, new_kv, prompt_key_value, step_key_value, parent_dev, parent_slot, cache_len, prompt_ids, score_weights):
    lanes_tp = lax.axis_size("tp")
    groups = lax.axis_size("grp") * lanes_tp
    vmem = pl.BlockSpec(memory_space=pltpu.VMEM)
    hbm = pl.BlockSpec(memory_space=pltpu.HBM)
    anywhere = pl.BlockSpec(memory_space=pl.ANY)
    table = pl.pallas_call(
        table_kernel,
        out_shape=jax.ShapeDtypeStruct((TAB, 128), I32),
        in_specs=[vmem] * 4,
        out_specs=vmem,
        compiler_params=pltpu.CompilerParams(vmem_limit_bytes=VMEM_LIMIT),
    )(parent_dev.reshape(8, 128), parent_slot.reshape(8, 128), cache_len.reshape(8, 128), prompt_ids.reshape(1, BEAMS))
    q = queries.reshape(BEAMS, ROWS, HEAD)
    kvn = jnp.pad(new_kv[0], ((0, 0), (0, NEWPAD - new_kv.shape[2]), (0, 0)))
    weights = score_weights.reshape(8, HEAD)
    dma = pltpu.SemaphoreType.DMA
    attended, score = pl.pallas_call(
        functools.partial(main_kernel, groups, lanes_tp),
        out_shape=(
            jax.ShapeDtypeStruct((BEAMS, ROWS, HEAD), BF16),
            jax.ShapeDtypeStruct((8, 128), F32),
        ),
        in_specs=[anywhere, vmem, vmem, vmem, hbm, hbm],
        out_specs=(vmem, vmem),
        scratch_shapes=[
            pltpu.SMEM((TAB, 128), I32),
            pltpu.VMEM((BEAMS, 128, 2 * HEAD), BF16),
        ] + [pltpu.VMEM((4, 2, SHARD, 2 * HEAD), BF16)] * 4 + [
            pltpu.VMEM((HOLD * CAP, ROWS, HEAD), BF16),
            pltpu.VMEM((HOLD * CAP, ROWS, HEAD), BF16),
            pltpu.VMEM((HOLD * CAP, ROWS, HEAD), BF16),
            pltpu.VMEM((HOLD * CAP, ROWS, HEAD), BF16),
            pltpu.VMEM((HOLD, 8, 128), F32),
            pltpu.VMEM((HOLD, 8, 128), F32),
            pltpu.VMEM((PLACES, ROWS, HEAD), BF16),
            pltpu.VMEM((PLACES, NEWPAD, 2 * HEAD), BF16),
            pltpu.VMEM((PLACES, ROWS, 2 * HEAD), F32),
            pltpu.VMEM((PLACES, ROWS, 128), F32),
            pltpu.VMEM((BEAMS, 128), F32),
            pltpu.VMEM((8, 128), F32),
            pltpu.VMEM((max(groups, 1), 8, 128), F32),
        ] + [dma((HOLD,))] * 6 + [dma((5,))] * 4 + [dma((8,))] * 2 + [dma((max(groups, 1),))] * 2 + [dma((3,))],
        compiler_params=pltpu.CompilerParams(
            collective_id=0, has_side_effects=True, vmem_limit_bytes=VMEM_LIMIT),
    )(table, q, kvn, weights, prompt_key_value[0], step_key_value[0])
    return attended.reshape(1, BEAMS, 4, 8 * HEAD), score[0, :BEAMS]


def solution(mesh):
    in_specs = (
        P("grp", "beam", None, "tp"),
        P("grp", "beam", None, "tp"),
        P("grp", None, "beam", "tp"),
        P("grp", "beam", None, "tp"),
        P(),
        P(),
        P(),
        P("beam"),
        P("grp", "tp"),
    )
    out_specs = (P("grp", "beam", None, "tp"), P("beam"))
    return jax.shard_map(on_device, mesh=mesh, in_specs=in_specs, out_specs=out_specs, check_vma=False)
```

```python
import functools
import math

import jax
import jax.numpy as jnp
from jax import lax
from jax.experimental import pallas as pl
from jax.experimental.pallas import tpu as pltpu
from jax.sharding import PartitionSpec as P

MESH = pl.DeviceIdType.MESH
F32, BF16, I32 = jnp.float32, jnp.bfloat16, jnp.int32

HEAD = 128
BEAMS = 64
ROWS = 32
CAP = 8
HOLD = 16
TILE = 8
TILES = BEAMS // TILE + 1
PLACES = TILES * TILE
TROWS = TILE * ROWS
SHARD = 256
NEW = 8
SCALE = math.log2(math.e) / math.sqrt(HEAD)
LOW = -1e30
VMEM_LIMIT = 61 * 1024 * 1024
TAB = 32
INV, PLACED, PROMPT, ARRIVAL, PLACE = 8, 24, 25, 26, 27


def iota(shape, axis):
    return lax.broadcasted_iota(I32, shape, axis)


def make_table(pdev_ref, slot_ref, length_ref, pid_ref, tab_ref):
    me = lax.axis_index("beam")
    z, x = lax.div(me, 2), lax.rem(me, 2)
    pdev = pdev_ref[...]
    code = (slot_ref[...] * 256 + length_ref[...]).astype(F32)

    a, b = iota((128, 128), 0), iota((128, 128), 1)
    upper = ((a < b) & ((a >> 6) == (b >> 6))).astype(F32)
    served = (pdev == me).astype(F32)
    rank = jnp.dot(served, upper, preferred_element_type=F32)
    lane = iota((8, 128), 1)
    head = jnp.zeros((8, 128), F32)
    for k in range(CAP):
        pick = jnp.where(rank == k, served, 0.0) * code
        for h in range(2):
            found = jnp.sum(jnp.where((lane >> 6) == h, pick, 0.0), axis=1, keepdims=True)
            head = jnp.where(lane == h * CAP + k, found, head)
    tab_ref[0:8, :] = head.astype(I32)

    upper = upper[:BEAMS, :BEAMS]
    pair = pdev_ref[pl.ds(z, 1), :]
    mine = jnp.where(x == 1, pair[:, BEAMS:], pair[:, :BEAMS])
    ahead = (((mine >> 1) - z) & 7) * 2 + ((mine - x) & 1)
    offset = iota((HOLD, BEAMS), 0)
    beam = iota((HOLD, BEAMS), 1).astype(F32)
    own = (jnp.broadcast_to(ahead, (HOLD, BEAMS)) == offset).astype(F32)
    own_rank = jnp.dot(own, upper, preferred_element_type=F32)
    lane = iota((HOLD, 128), 1)
    body = jnp.zeros((HOLD, 128), F32)
    for k in range(CAP):
        found = jnp.sum(jnp.where(own_rank == k, own, 0.0) * beam, axis=1, keepdims=True)
        body = jnp.where(lane == k, found, body)
    tab_ref[8:8 + HOLD, :] = body.astype(I32)

    arrival = jnp.sum(own * (offset.astype(F32) * CAP + jnp.minimum(own_rank, CAP - 1)), axis=0, keepdims=True)
    first = (pid_ref[...] == 0).astype(F32)
    before = jnp.dot(jnp.broadcast_to(first, (8, BEAMS)), upper, preferred_element_type=F32)[0:1]
    count = jnp.sum(first, axis=1, keepdims=True).astype(I32)
    filled = (count + (TILE - 1)) & (-TILE)
    after = filled.astype(F32) + iota((1, BEAMS), 1).astype(F32) - before
    place = jnp.where(first > 0.5, before, after)
    diagonal = iota((BEAMS, BEAMS), 0) == iota((BEAMS, BEAMS), 1)
    column = jnp.sum(jnp.where(diagonal, place, 0.0), axis=1, keepdims=True)
    there = column == iota((BEAMS, 128), 1).astype(F32)
    holder = jnp.sum(jnp.where(there, iota((BEAMS, 128), 0).astype(F32), 0.0), axis=0, keepdims=True)
    which = (iota((1, 128), 1) * TILE >= filled).astype(F32)
    rest = jnp.zeros((1, 128 - BEAMS), F32)
    tail = jnp.concatenate([
        holder, which, jnp.concatenate([arrival, rest], axis=1), jnp.concatenate([place, rest], axis=1),
        jnp.zeros((4, 128), F32)], axis=0)
    tab_ref[24:32, :] = tail.astype(I32)


OWN, XOWN, ANTI, XANTI = 0, 1, 14, 15
FWD = {1: 2, 2: 6, 3: 10}
BWD = {1: 3, 2: 7, 3: 11}
XFWD = {1: 4, 2: 8, 3: 12}
XBWD = {1: 5, 2: 9, 3: 13}


def dot_nt(a, b):
    return lax.dot_general(a, b, (((1,), (1,)), ((), ())), preferred_element_type=F32)


def dot_nn(a, b):
    return lax.dot_general(a, b, (((1,), (0,)), ((), ())), preferred_element_type=F32)


def main_kernel(
    groups, lanes_tp, pdev_ref, slot_ref, length_ref, pid_ref, w_ref, q_hbm, kvn_hbm, prompt_hbm, pages_hbm,
    out_ref, score_ref,
    table, tab, q_ref, kvn_ref, pages, kv0, kv1, kv2, kv3, kv4, send, recv, ret_out, ret_in, stat_out, stat_in,
    qt, kvt, acc, high, part, share, shares,
    q_ss, q_rs, r_ss, r_rs, s_ss, s_rs, f_ss, f_rs, b_ss, b_rs, x_ss, x_rs, c_ss, c_rs, l_sem,
):
    me = lax.axis_index("beam")
    grp = lax.axis_index("grp")
    tp = lax.axis_index("tp")
    group = grp * lanes_tp + tp
    z, x = lax.div(me, 2), lax.rem(me, 2)

    def at(dz, dx):
        return lax.rem(z + dz + 8, 8) * 2 + lax.rem(x + dx, 2)

    def target(o):
        return at(lax.div(o, 2), lax.rem(o, 2))

    def origin(o):
        return at(-lax.div(o, 2), lax.rem(o, 2))

    def near(i):
        g, r = lax.div(i - 1, 4), lax.rem(i - 1, 4)
        return (g + 1 + lax.div(r, 2) * (6 - 2 * g)) * 2 + lax.rem(r, 2)

    up, down, side = at(1, 0), at(-1, 0), at(0, 1)

    held = (kv0, kv1, kv2, kv3, kv4)

    def shard_at(slot):
        if slot == XANTI:
            return kv4.at[0]
        return held[slot // 4].at[slot % 4]

    load_prompt = pltpu.make_async_copy(prompt_hbm, shard_at(OWN), l_sem.at[0])
    load_pages = pltpu.make_async_copy(pages_hbm, pages, l_sem.at[1])
    load_queries = pltpu.make_async_copy(q_hbm, q_ref, l_sem.at[3])
    load_new = pltpu.make_async_copy(kvn_hbm, kvn_ref, l_sem.at[4])
    for load in (load_prompt, load_queries, load_new, load_pages):
        load.start()

    barrier = pltpu.get_barrier_semaphore()

    def greet_beam(o, _):
        pl.semaphore_signal(barrier, inc=1, device_id={"beam": lax.rem(me + o, HOLD)}, device_id_type=MESH)
        return 0

    lax.fori_loop(1, HOLD, greet_beam, 0)

    def group_peer(o):
        peer = lax.rem(group + o, groups)
        return {"grp": lax.div(peer, lanes_tp), "tp": lax.rem(peer, lanes_tp)}

    if groups > 1:
        def greet_group(o, _):
            pl.semaphore_signal(barrier, inc=1, device_id=group_peer(o), device_id_type=MESH)
            return 0

        lax.fori_loop(1, groups, greet_group, 0)

    def shard_copy(src, dst, to, ss, rs, half=None):
        a, b = shard_at(src), shard_at(dst)
        if half is not None:
            a, b = a.at[half], b.at[half]
        return pltpu.make_async_remote_copy(
            src_ref=a, dst_ref=b, send_sem=ss, recv_sem=rs, device_id={"beam": to}, device_id_type=MESH)

    def fwd_copy(s):
        src = OWN if s == 1 else FWD[s - 1]
        if s == 4:
            return shard_copy(src, ANTI, up, f_ss.at[s], f_rs.at[s], 0)
        return shard_copy(src, FWD[s], up, f_ss.at[s], f_rs.at[s])

    def bwd_copy(s):
        src = OWN if s == 1 else BWD[s - 1]
        if s == 4:
            return shard_copy(src, ANTI, down, b_ss.at[s], b_rs.at[s], 1)
        return shard_copy(src, BWD[s], down, b_ss.at[s], b_rs.at[s])

    x_plan = [(OWN, XOWN)]
    for s in (1, 2, 3):
        x_plan += [(FWD[s], XFWD[s]), (BWD[s], XBWD[s])]
    x_plan += [(ANTI, XANTI)]

    def x_copy(i):
        src, dst = x_plan[i]
        return shard_copy(src, dst, side, x_ss.at[i], x_rs.at[i])

    load_prompt.wait()
    pl.semaphore_wait(barrier, HOLD - 1 + groups - 1)
    fwd_copy(1).start()
    bwd_copy(1).start()
    x_copy(0).start()

    make_table(pdev_ref, slot_ref, length_ref, pid_ref, table)
    load_table = pltpu.make_async_copy(table, tab, l_sem.at[2])
    load_table.start()
    load_table.wait()

    load_queries.wait()
    def span(o):
        return pl.ds(o * CAP, CAP)

    def pack(o, into):
        for k in range(CAP):
            into[o * CAP + k] = q_ref[tab[INV + o, k] & (BEAMS - 1)]


    def query_copy(o):
        return pltpu.make_async_remote_copy(
            src_ref=send.at[span(o)], dst_ref=recv.at[span(o)], send_sem=q_ss.at[o], recv_sem=q_rs.at[o],
            device_id={"beam": target(o)}, device_id_type=MESH)

    def send_near(i, _):
        o = near(i)
        pack(o, send)
        query_copy(o).start()
        return 0

    pack(1, send)
    query_copy(1).start()
    lax.fori_loop(1, 5, send_near, 0)
    pack(0, recv)
    load_new.wait()

    def ring_step(s):
        fwd_copy(s).wait_recv()
        if s < 4:
            fwd_copy(s + 1).start()
            x_copy(2 * s - 1).start()
        bwd_copy(s).wait_recv()
        if s < 4:
            bwd_copy(s + 1).start()
            x_copy(2 * s).start()
        else:
            x_copy(7).start()

    def fill_tile(t, _):
        for i in range(TILE):
            b = tab[PLACED, t * TILE + i] & (BEAMS - 1)
            qt[t * TILE + i] = q_ref[b]
            kvt[t * TILE + i] = kvn_ref[b].astype(F32)
        return 0

    lax.fori_loop(0, TILES, fill_tile, 0)

    def with_ones(values):
        return jnp.concatenate([values, jnp.ones(values.shape, BF16)], axis=1)

    diag = (iota((TROWS, 128), 0) & 127) == iota((TROWS, 128), 1)
    column = iota((ROWS, 128), 1)

    def step_part(o, into_out, into_stat):
        c = origin(o)
        row, lane = lax.div(c, 2), lax.rem(c, 2) * CAP
        blocks = []
        values = []
        for j in range(CAP // 2):
            k0 = 2 * j
            code0, code1 = tab[row, lane + k0], tab[row, lane + k0 + 1]
            page0, page1 = pages[(code0 >> 8) & (BEAMS - 1)], pages[(code1 >> 8) & (BEAMS - 1)]
            keys = jnp.concatenate([page0[:, :HEAD], page1[:, :HEAD]], axis=0)
            values.append(with_ones(jnp.concatenate([page0[:, HEAD:], page1[:, HEAD:]], axis=0)))
            queries = recv[pl.ds(o * CAP + k0, 2)].reshape(2 * ROWS, HEAD)
            s = dot_nt(queries, keys)
            blocks.append(jnp.where(column < (code0 & 255), s[:ROWS, :128] * SCALE, LOW))
            blocks.append(jnp.where(column < (code1 & 255), s[ROWS:, 128:] * SCALE, LOW))
        s = jnp.concatenate(blocks, axis=0)
        top = jnp.max(s, axis=1, keepdims=True)
        p = jnp.exp2(s - top).astype(BF16)
        zero = jnp.zeros((ROWS, 128), BF16)
        sums = []
        for j in range(CAP // 2):
            p0, p1 = p[2 * j * ROWS:(2 * j + 1) * ROWS], p[(2 * j + 1) * ROWS:(2 * j + 2) * ROWS]
            wide = jnp.concatenate(
                [jnp.concatenate([p0, zero], axis=1), jnp.concatenate([zero, p1], axis=1)], axis=0)
            sums.append(dot_nn(wide, values[j]))
        sums = jnp.concatenate(sums, axis=0)
        total = sums[:, HEAD:]
        into_out[span(o)] = (sums[:, :HEAD] / total).astype(BF16).reshape(CAP, ROWS, HEAD)
        level = top + jnp.log2(total)
        flat = jnp.sum(jnp.where(diag, level, 0.0).reshape(2, 128, 128), axis=1)
        into_stat[o] = flat

    def back_copy(o):
        to = {"beam": origin(o)}
        return (
            pltpu.make_async_remote_copy(
                src_ref=ret_out.at[span(o)], dst_ref=ret_in.at[span(o)], send_sem=r_ss.at[o],
                recv_sem=r_rs.at[o], device_id=to, device_id_type=MESH),
            pltpu.make_async_remote_copy(
                src_ref=stat_out.at[o], dst_ref=stat_in.at[o], send_sem=s_ss.at[o],
                recv_sem=s_rs.at[o], device_id=to, device_id_type=MESH),
        )

    def serve(i, _):
        o = near(i)
        query_copy(o).wait_recv()
        step_part(o, ret_out, stat_out)
        for copy in back_copy(o):
            copy.start()
        return 0

    def new_part(t, _):
        q = qt[pl.ds(t * TILE, TILE)].reshape(TROWS, HEAD)
        kv = kvt[pl.ds(t * TILE, TILE)].reshape(TILE * NEW, HEAD)
        kv = jnp.concatenate([kv, jnp.zeros(kv.shape, F32)], axis=0).astype(BF16)
        row, col = iota((TROWS, 128), 0), iota((TROWS, 128), 1)
        seen = ((row >> 5) == (col >> 3)) & ((col & 7) <= (row & 3))
        s = jnp.where(seen, dot_nt(q, kv) * SCALE, LOW)
        top = jnp.max(s, axis=1, keepdims=True)
        p = pltpu.roll(jnp.exp2(s - top), 4, 1).astype(BF16)
        acc[pl.ds(t * TILE, TILE)] = dot_nn(p, with_ones(kv)).reshape(TILE, ROWS, 2 * HEAD)
        high[pl.ds(t * TILE, TILE)] = jnp.broadcast_to(top, (TROWS, 128)).reshape(TILE, ROWS, 128)
        return 0

    def prompt_part(number):
        keys = held[number].shape[0] * SHARD

        def one(t):
            own = tab[PROMPT, t] & 1
            q = qt[pl.ds(t * TILE, TILE)].reshape(TROWS, HEAD)
            kv = held[number][:, own].reshape(keys, 2 * HEAD)
            s = dot_nt(q, kv[:, :HEAD])
            cols = [s[:, i * 128:(i + 1) * 128] for i in range(keys // 128)]
            top = functools.reduce(jnp.maximum, cols)
            old = high[pl.ds(t * TILE, TILE)].reshape(TROWS, 128)
            top = jnp.maximum(old, jnp.max(top, axis=1, keepdims=True) * SCALE)
            p = jnp.concatenate([jnp.exp2(col * SCALE - top).astype(BF16) for col in cols], axis=1)
            fade = jnp.exp2(old - top)
            add = dot_nn(p, with_ones(kv[:, HEAD:]))
            was = acc[pl.ds(t * TILE, TILE)].reshape(TROWS, 2 * HEAD)
            new = was * jnp.concatenate([fade, fade], axis=1) + add
            acc[pl.ds(t * TILE, TILE)] = new.reshape(TILE, ROWS, 2 * HEAD)
            high[pl.ds(t * TILE, TILE)] = top.reshape(TILE, ROWS, 128)

        def some(i, _):
            for u in range(3):
                one(i * 3 + u)
            return 0

        lax.fori_loop(0, TILES // 3, some, 0)

    def query_first(_):
        query_copy(1).wait_recv()
        step_part(1, ret_out, stat_out)
        for copy in back_copy(1):
            copy.start()

    load_pages.wait()
    step_part(0, ret_in, stat_in)
    lax.fori_loop(0, TILES, new_part, 0)
    ring_step(1)
    lax.fori_loop(5, 9, send_near, 0)
    ring_step(2)
    lax.fori_loop(9, 15, send_near, 0)
    query_first(0)
    lax.fori_loop(1, 5, serve, 0)
    ring_step(3)
    lax.fori_loop(5, 9, serve, 0)
    ring_step(4)
    lax.fori_loop(9, 15, serve, 0)
    x_copy(0).wait_recv()
    prompt_part(0)
    for i in (1, 2):
        x_copy(i).wait_recv()
    prompt_part(1)
    for i in (3, 4):
        x_copy(i).wait_recv()
    prompt_part(2)
    for i in (5, 6):
        x_copy(i).wait_recv()
    prompt_part(3)
    x_copy(7).wait_recv()
    prompt_part(4)

    def await_back(o, _):
        for copy in back_copy(o):
            copy.wait_recv()
        return 0

    lax.fori_loop(1, HOLD, await_back, 0)

    lane_of = iota((ROWS, 128), 1) - iota((ROWS, 128), 0)

    head_of = iota((ROWS, 128), 0) >> 2
    weights = jnp.zeros((ROWS, 128), F32)
    for j in range(8):
        weights = jnp.where(head_of == j, w_ref[j:j + 1, :], weights)

    def finish(i, _):
        for u in range(4):
            b = i * 4 + u
            a = tab[ARRIVAL, b] & (HOLD * CAP - 1)
            place = jnp.clip(tab[PLACE, b], 0, PLACES - 1)
            line = stat_in[a >> 3, pl.ds((a >> 2) & 1, 1), :]
            level = jnp.sum(jnp.where(lane_of == (a & 3) * ROWS, line, 0.0), axis=1, keepdims=True)
            old = high[place]
            top = jnp.maximum(old, level)
            mine, theirs = jnp.exp2(old - top), jnp.exp2(level - top)
            sums = acc[place]
            whole = sums[:, :HEAD] * mine + ret_in[a].astype(F32) * theirs
            result = (whole / (sums[:, HEAD:] * mine + theirs)).astype(BF16)
            out_ref[b] = result
            part[pl.ds(b, 1), :] = jnp.sum(result.astype(F32) * weights, axis=0, keepdims=True)
        return 0

    lax.fori_loop(0, BEAMS // 4, finish, 0)

    score = jnp.sum(part[...], axis=1, keepdims=True)
    spot = iota((BEAMS, 128), 0) == iota((BEAMS, 128), 1)
    line = jnp.sum(jnp.where(spot, score, 0.0), axis=0, keepdims=True) * 0.25
    share[...] = jnp.broadcast_to(line, (8, 128))
    if groups > 1:
        def share_copy(o):
            return pltpu.make_async_remote_copy(
                src_ref=share, dst_ref=shares.at[group], send_sem=c_ss.at[o], recv_sem=c_rs.at[o],
                device_id=group_peer(o), device_id_type=MESH)

        def send_share(o, _):
            share_copy(o).start()
            return 0

        lax.fori_loop(1, groups, send_share, 0)
        shares[group] = share[...]

        def await_share(o, _):
            share_copy(o).wait()
            return 0

        lax.fori_loop(1, groups, await_share, 0)
        score_ref[...] = jnp.sum(shares[...], axis=0)
    else:
        score_ref[...] = share[...]

    def await_sends(o, _):
        query_copy(o).wait_send()
        for copy in back_copy(o):
            copy.wait_send()
        return 0

    lax.fori_loop(1, HOLD, await_sends, 0)
    for s in (1, 2, 3, 4):
        fwd_copy(s).wait_send()
        bwd_copy(s).wait_send()
    for i in range(8):
        x_copy(i).wait_send()


def on_device(queries, new_kv, prompt_key_value, step_key_value, parent_dev, parent_slot, cache_len, prompt_ids, score_weights):
    lanes_tp = lax.axis_size("tp")
    groups = lax.axis_size("grp") * lanes_tp
    vmem = pl.BlockSpec(memory_space=pltpu.VMEM)
    hbm = pl.BlockSpec(memory_space=pltpu.HBM)
    q = queries.reshape(BEAMS, 4, 8, HEAD).transpose(0, 2, 1, 3).reshape(BEAMS, ROWS, HEAD)
    kvn = new_kv.reshape(BEAMS, 4, 2, HEAD).transpose(0, 2, 1, 3).reshape(BEAMS, NEW, HEAD)
    weights = score_weights.reshape(8, HEAD)
    dma = pltpu.SemaphoreType.DMA
    attended, score = pl.pallas_call(
        functools.partial(main_kernel, groups, lanes_tp),
        out_shape=(
            jax.ShapeDtypeStruct((BEAMS, ROWS, HEAD), BF16),
            jax.ShapeDtypeStruct((8, 128), F32),
        ),
        in_specs=[vmem] * 5 + [hbm] * 4,
        out_specs=(vmem, vmem),
        scratch_shapes=[
            pltpu.VMEM((TAB, 128), I32),
            pltpu.SMEM((TAB, 128), I32),
            pltpu.VMEM((BEAMS, ROWS, HEAD), BF16),
            pltpu.VMEM((BEAMS, NEW, HEAD), BF16),
            pltpu.VMEM((BEAMS, 128, 2 * HEAD), BF16),
        ] + [pltpu.VMEM((n, 2, SHARD, 2 * HEAD), BF16) for n in (4, 4, 4, 3, 1)] + [
            pltpu.VMEM((HOLD * CAP, ROWS, HEAD), BF16),
            pltpu.VMEM((HOLD * CAP, ROWS, HEAD), BF16),
            pltpu.VMEM((HOLD * CAP, ROWS, HEAD), BF16),
            pltpu.VMEM((HOLD * CAP, ROWS, HEAD), BF16),
            pltpu.VMEM((HOLD, 2, 128), F32),
            pltpu.VMEM((HOLD, 2, 128), F32),
            pltpu.VMEM((PLACES, ROWS, HEAD), BF16),
            pltpu.VMEM((PLACES, NEW, HEAD), F32),
            pltpu.VMEM((PLACES, ROWS, 2 * HEAD), F32),
            pltpu.VMEM((PLACES, ROWS, 128), F32),
            pltpu.VMEM((BEAMS, 128), F32),
            pltpu.VMEM((8, 128), F32),
            pltpu.VMEM((max(groups, 1), 8, 128), F32),
        ] + [dma((HOLD,))] * 6 + [dma((5,))] * 4 + [dma((8,))] * 2 + [dma((max(groups, 1),))] * 2 + [dma((5,))],
        compiler_params=pltpu.CompilerParams(
            collective_id=0, has_side_effects=True, vmem_limit_bytes=VMEM_LIMIT),
    )(parent_dev.reshape(8, 128), parent_slot.reshape(8, 128), cache_len.reshape(8, 128), prompt_ids.reshape(1, BEAMS),
      weights, q, kvn, prompt_key_value[0], step_key_value[0])
    attended = attended.reshape(BEAMS, 8, 4, HEAD).transpose(0, 2, 1, 3)
    return attended.reshape(1, BEAMS, 4, 8 * HEAD), score[0, :BEAMS]


def solution(mesh):
    in_specs = (
        P("grp", "beam", None, "tp"),
        P("grp", "beam", None, "tp"),
        P("grp", None, "beam", "tp"),
        P("grp", "beam", None, "tp"),
        P(),
        P(),
        P(),
        P("beam"),
        P("grp", "tp"),
    )
    out_specs = (P("grp", "beam", None, "tp"), P("beam"))
    return jax.shard_map(on_device, mesh=mesh, in_specs=in_specs, out_specs=out_specs, check_vma=False)
```

```python
import functools
import math

import jax
import jax.numpy as jnp
from jax import lax
from jax.experimental import pallas as pl
from jax.experimental.pallas import tpu as pltpu
from jax.sharding import PartitionSpec as P

MESH = pl.DeviceIdType.MESH
F32, BF16, I32 = jnp.float32, jnp.bfloat16, jnp.int32

HEAD = 128
BEAMS = 64
ROWS = 32
CAP = 8
HOLD = 16
TILE = 8
TILES = BEAMS // TILE + 1
PLACES = TILES * TILE
TROWS = TILE * ROWS
SHARD = 256
NEW = 8
SCALE = math.log2(math.e) / math.sqrt(HEAD)
LOW = -1e30
VMEM_LIMIT = 61 * 1024 * 1024
TAB = 32
INV, PLACED, PROMPT, ARRIVAL, PLACE = 8, 24, 25, 26, 27


def iota(shape, axis):
    return lax.broadcasted_iota(I32, shape, axis)


def make_table(pdev_ref, slot_ref, length_ref, pid_ref, tab_ref):
    me = lax.axis_index("beam")
    z, x = lax.div(me, 2), lax.rem(me, 2)
    pdev = pdev_ref[...]
    code = (slot_ref[...] * 256 + length_ref[...]).astype(F32)

    a, b = iota((128, 128), 0), iota((128, 128), 1)
    upper = ((a < b) & ((a >> 6) == (b >> 6))).astype(F32)
    served = (pdev == me).astype(F32)
    rank = jnp.dot(served, upper, preferred_element_type=F32)
    lane = iota((8, 128), 1)
    head = jnp.zeros((8, 128), F32)
    for k in range(CAP):
        pick = jnp.where(rank == k, served, 0.0) * code
        for h in range(2):
            found = jnp.sum(jnp.where((lane >> 6) == h, pick, 0.0), axis=1, keepdims=True)
            head = jnp.where(lane == h * CAP + k, found, head)
    tab_ref[0:8, :] = head.astype(I32)

    upper = upper[:BEAMS, :BEAMS]
    pair = pdev_ref[pl.ds(z, 1), :]
    mine = jnp.where(x == 1, pair[:, BEAMS:], pair[:, :BEAMS])
    ahead = (((mine >> 1) - z) & 7) * 2 + ((mine - x) & 1)
    offset = iota((HOLD, BEAMS), 0)
    beam = iota((HOLD, BEAMS), 1).astype(F32)
    own = (jnp.broadcast_to(ahead, (HOLD, BEAMS)) == offset).astype(F32)
    own_rank = jnp.dot(own, upper, preferred_element_type=F32)
    lane = iota((HOLD, 128), 1)
    body = jnp.zeros((HOLD, 128), F32)
    for k in range(CAP):
        found = jnp.sum(jnp.where(own_rank == k, own, 0.0) * beam, axis=1, keepdims=True)
        body = jnp.where(lane == k, found, body)
    tab_ref[8:8 + HOLD, :] = body.astype(I32)

    arrival = jnp.sum(own * (offset.astype(F32) * CAP + jnp.minimum(own_rank, CAP - 1)), axis=0, keepdims=True)
    first = (pid_ref[...] == 0).astype(F32)
    before = jnp.dot(jnp.broadcast_to(first, (8, BEAMS)), upper, preferred_element_type=F32)[0:1]
    count = jnp.sum(first, axis=1, keepdims=True).astype(I32)
    filled = (count + (TILE - 1)) & (-TILE)
    after = filled.astype(F32) + iota((1, BEAMS), 1).astype(F32) - before
    place = jnp.where(first > 0.5, before, after)
    diagonal = iota((BEAMS, BEAMS), 0) == iota((BEAMS, BEAMS), 1)
    column = jnp.sum(jnp.where(diagonal, place, 0.0), axis=1, keepdims=True)
    there = column == iota((BEAMS, 128), 1).astype(F32)
    holder = jnp.sum(jnp.where(there, iota((BEAMS, 128), 0).astype(F32), 0.0), axis=0, keepdims=True)
    which = (iota((1, 128), 1) * TILE >= filled).astype(F32)
    rest = jnp.zeros((1, 128 - BEAMS), F32)
    tail = jnp.concatenate([
        holder, which, jnp.concatenate([arrival, rest], axis=1), jnp.concatenate([place, rest], axis=1),
        jnp.zeros((4, 128), F32)], axis=0)
    tab_ref[24:32, :] = tail.astype(I32)


OWN, XOWN, ANTI, XANTI = 0, 1, 14, 15
FWD = {1: 2, 2: 6, 3: 10}
BWD = {1: 3, 2: 7, 3: 11}
XFWD = {1: 4, 2: 8, 3: 12}
XBWD = {1: 5, 2: 9, 3: 13}


def dot_nt(a, b):
    return lax.dot_general(a, b, (((1,), (1,)), ((), ())), preferred_element_type=F32)


def dot_nn(a, b):
    return lax.dot_general(a, b, (((1,), (0,)), ((), ())), preferred_element_type=F32)


def main_kernel(
    groups, lanes_tp, pdev_hbm, slot_hbm, length_hbm, pid_hbm, w_hbm, q_hbm, kvn_hbm, prompt_hbm, pages_hbm,
    out_ref, score_ref,
    pdev_ref, slot_ref, length_ref, pid_ref, w_ref, table, tab, q_ref, kvn_ref, pages, kv0, kv1, kv2, kv3, kv4, send, recv, ret_out, ret_in, stat_out, stat_in,
    qt, kvt, acc, high, part, share, shares,
    q_ss, q_rs, r_ss, r_rs, s_ss, s_rs, f_ss, f_rs, b_ss, b_rs, x_ss, x_rs, c_ss, c_rs, l_sem,
):
    me = lax.axis_index("beam")
    grp = lax.axis_index("grp")
    tp = lax.axis_index("tp")
    group = grp * lanes_tp + tp
    z, x = lax.div(me, 2), lax.rem(me, 2)

    def at(dz, dx):
        return lax.rem(z + dz + 8, 8) * 2 + lax.rem(x + dx, 2)

    def target(o):
        return at(lax.div(o, 2), lax.rem(o, 2))

    def origin(o):
        return at(-lax.div(o, 2), lax.rem(o, 2))

    def near(i):
        g, r = lax.div(i - 1, 4), lax.rem(i - 1, 4)
        return (g + 1 + lax.div(r, 2) * (6 - 2 * g)) * 2 + lax.rem(r, 2)

    up, down, side = at(1, 0), at(-1, 0), at(0, 1)

    held = (kv0, kv1, kv2, kv3, kv4)

    def shard_at(slot):
        if slot == XANTI:
            return kv4.at[0]
        return held[slot // 4].at[slot % 4]

    load_prompt = pltpu.make_async_copy(prompt_hbm, shard_at(OWN), l_sem.at[0])
    load_pages = pltpu.make_async_copy(pages_hbm, pages, l_sem.at[1])
    load_queries = pltpu.make_async_copy(q_hbm, q_ref, l_sem.at[3])
    load_new = pltpu.make_async_copy(kvn_hbm, kvn_ref, l_sem.at[4])
    load_small = [
        pltpu.make_async_copy(src, dst, l_sem.at[5 + i])
        for i, (src, dst) in enumerate((
            (pdev_hbm, pdev_ref), (slot_hbm, slot_ref), (length_hbm, length_ref), (pid_hbm, pid_ref), (w_hbm, w_ref)))]
    load_prompt.start()

    barrier = pltpu.get_barrier_semaphore()

    def greet_beam(o, _):
        pl.semaphore_signal(barrier, inc=1, device_id={"beam": lax.rem(me + o, HOLD)}, device_id_type=MESH)
        return 0

    lax.fori_loop(1, HOLD, greet_beam, 0)

    def group_peer(o):
        peer = lax.rem(group + o, groups)
        return {"grp": lax.div(peer, lanes_tp), "tp": lax.rem(peer, lanes_tp)}

    if groups > 1:
        def greet_group(o, _):
            pl.semaphore_signal(barrier, inc=1, device_id=group_peer(o), device_id_type=MESH)
            return 0

        lax.fori_loop(1, groups, greet_group, 0)

    def shard_copy(src, dst, to, ss, rs, half=None):
        a, b = shard_at(src), shard_at(dst)
        if half is not None:
            a, b = a.at[half], b.at[half]
        return pltpu.make_async_remote_copy(
            src_ref=a, dst_ref=b, send_sem=ss, recv_sem=rs, device_id={"beam": to}, device_id_type=MESH)

    def fwd_copy(s):
        src = OWN if s == 1 else FWD[s - 1]
        if s == 4:
            return shard_copy(src, ANTI, up, f_ss.at[s], f_rs.at[s], 0)
        return shard_copy(src, FWD[s], up, f_ss.at[s], f_rs.at[s])

    def bwd_copy(s):
        src = OWN if s == 1 else BWD[s - 1]
        if s == 4:
            return shard_copy(src, ANTI, down, b_ss.at[s], b_rs.at[s], 1)
        return shard_copy(src, BWD[s], down, b_ss.at[s], b_rs.at[s])

    x_plan = [(OWN, XOWN)]
    for s in (1, 2, 3):
        x_plan += [(FWD[s], XFWD[s]), (BWD[s], XBWD[s])]
    x_plan += [(ANTI, XANTI)]

    def x_copy(i):
        src, dst = x_plan[i]
        return shard_copy(src, dst, side, x_ss.at[i], x_rs.at[i])

    for load in load_small + [load_queries, load_new, load_pages]:
        load.start()
    load_prompt.wait()
    pl.semaphore_wait(barrier, HOLD - 1 + groups - 1)
    fwd_copy(1).start()
    bwd_copy(1).start()
    x_copy(0).start()

    for load in load_small:
        load.wait()
    make_table(pdev_ref, slot_ref, length_ref, pid_ref, table)
    load_table = pltpu.make_async_copy(table, tab, l_sem.at[2])
    load_table.start()
    load_table.wait()

    load_queries.wait()
    def span(o):
        return pl.ds(o * CAP, CAP)

    def pack(o, into):
        for k in range(CAP):
            into[o * CAP + k] = q_ref[tab[INV + o, k] & (BEAMS - 1)]


    def query_copy(o):
        return pltpu.make_async_remote_copy(
            src_ref=send.at[span(o)], dst_ref=recv.at[span(o)], send_sem=q_ss.at[o], recv_sem=q_rs.at[o],
            device_id={"beam": target(o)}, device_id_type=MESH)

    def send_near(i, _):
        o = near(i)
        pack(o, send)
        query_copy(o).start()
        return 0

    pack(1, send)
    query_copy(1).start()
    lax.fori_loop(1, 5, send_near, 0)
    pack(0, recv)
    load_new.wait()

    def ring_step(s):
        fwd_copy(s).wait_recv()
        if s < 4:
            fwd_copy(s + 1).start()
            x_copy(2 * s - 1).start()
        bwd_copy(s).wait_recv()
        if s < 4:
            bwd_copy(s + 1).start()
            x_copy(2 * s).start()
        else:
            x_copy(7).start()

    def fill_tile(t, _):
        for i in range(TILE):
            b = tab[PLACED, t * TILE + i] & (BEAMS - 1)
            qt[t * TILE + i] = q_ref[b]
            kvt[t * TILE + i] = kvn_ref[b].astype(F32)
        return 0

    lax.fori_loop(0, TILES, fill_tile, 0)

    def with_ones(values):
        return jnp.concatenate([values, jnp.ones(values.shape, BF16)], axis=1)

    diag = (iota((TROWS, 128), 0) & 127) == iota((TROWS, 128), 1)
    column = iota((ROWS, 128), 1)

    def step_part(o, into_out, into_stat):
        c = origin(o)
        row, lane = lax.div(c, 2), lax.rem(c, 2) * CAP
        blocks = []
        values = []
        for j in range(CAP // 2):
            k0 = 2 * j
            code0, code1 = tab[row, lane + k0], tab[row, lane + k0 + 1]
            page0, page1 = pages[(code0 >> 8) & (BEAMS - 1)], pages[(code1 >> 8) & (BEAMS - 1)]
            keys = jnp.concatenate([page0[:, :HEAD], page1[:, :HEAD]], axis=0)
            values.append(with_ones(jnp.concatenate([page0[:, HEAD:], page1[:, HEAD:]], axis=0)))
            queries = recv[pl.ds(o * CAP + k0, 2)].reshape(2 * ROWS, HEAD)
            s = dot_nt(queries, keys)
            blocks.append(jnp.where(column < (code0 & 255), s[:ROWS, :128] * SCALE, LOW))
            blocks.append(jnp.where(column < (code1 & 255), s[ROWS:, 128:] * SCALE, LOW))
        s = jnp.concatenate(blocks, axis=0)
        top = jnp.max(s, axis=1, keepdims=True)
        p = jnp.exp2(s - top).astype(BF16)
        zero = jnp.zeros((ROWS, 128), BF16)
        sums = []
        for j in range(CAP // 2):
            p0, p1 = p[2 * j * ROWS:(2 * j + 1) * ROWS], p[(2 * j + 1) * ROWS:(2 * j + 2) * ROWS]
            wide = jnp.concatenate(
                [jnp.concatenate([p0, zero], axis=1), jnp.concatenate([zero, p1], axis=1)], axis=0)
            sums.append(dot_nn(wide, values[j]))
        sums = jnp.concatenate(sums, axis=0)
        total = sums[:, HEAD:]
        into_out[span(o)] = (sums[:, :HEAD] / total).astype(BF16).reshape(CAP, ROWS, HEAD)
        level = top + jnp.log2(total)
        flat = jnp.sum(jnp.where(diag, level, 0.0).reshape(2, 128, 128), axis=1)
        into_stat[o] = flat

    def back_copy(o):
        to = {"beam": origin(o)}
        return (
            pltpu.make_async_remote_copy(
                src_ref=ret_out.at[span(o)], dst_ref=ret_in.at[span(o)], send_sem=r_ss.at[o],
                recv_sem=r_rs.at[o], device_id=to, device_id_type=MESH),
            pltpu.make_async_remote_copy(
                src_ref=stat_out.at[o], dst_ref=stat_in.at[o], send_sem=s_ss.at[o],
                recv_sem=s_rs.at[o], device_id=to, device_id_type=MESH),
        )

    def serve(i, _):
        o = near(i)
        query_copy(o).wait_recv()
        step_part(o, ret_out, stat_out)
        for copy in back_copy(o):
            copy.start()
        return 0

    def new_part(t, _):
        q = qt[pl.ds(t * TILE, TILE)].reshape(TROWS, HEAD)
        kv = kvt[pl.ds(t * TILE, TILE)].reshape(TILE * NEW, HEAD)
        kv = jnp.concatenate([kv, jnp.zeros(kv.shape, F32)], axis=0).astype(BF16)
        row, col = iota((TROWS, 128), 0), iota((TROWS, 128), 1)
        seen = ((row >> 5) == (col >> 3)) & ((col & 7) <= (row & 3))
        s = jnp.where(seen, dot_nt(q, kv) * SCALE, LOW)
        top = jnp.max(s, axis=1, keepdims=True)
        p = pltpu.roll(jnp.exp2(s - top), 4, 1).astype(BF16)
        acc[pl.ds(t * TILE, TILE)] = dot_nn(p, with_ones(kv)).reshape(TILE, ROWS, 2 * HEAD)
        high[pl.ds(t * TILE, TILE)] = jnp.broadcast_to(top, (TROWS, 128)).reshape(TILE, ROWS, 128)
        return 0

    def prompt_part(number):
        keys = held[number].shape[0] * SHARD

        def one(t):
            own = tab[PROMPT, t] & 1
            q = qt[pl.ds(t * TILE, TILE)].reshape(TROWS, HEAD)
            kv = held[number][:, own].reshape(keys, 2 * HEAD)
            s = dot_nt(q, kv[:, :HEAD])
            cols = [s[:, i * 128:(i + 1) * 128] for i in range(keys // 128)]
            top = functools.reduce(jnp.maximum, cols)
            old = high[pl.ds(t * TILE, TILE)].reshape(TROWS, 128)
            top = jnp.maximum(old, jnp.max(top, axis=1, keepdims=True) * SCALE)
            p = jnp.concatenate([jnp.exp2(col * SCALE - top).astype(BF16) for col in cols], axis=1)
            fade = jnp.exp2(old - top)
            add = dot_nn(p, with_ones(kv[:, HEAD:]))
            was = acc[pl.ds(t * TILE, TILE)].reshape(TROWS, 2 * HEAD)
            new = was * jnp.concatenate([fade, fade], axis=1) + add
            acc[pl.ds(t * TILE, TILE)] = new.reshape(TILE, ROWS, 2 * HEAD)
            high[pl.ds(t * TILE, TILE)] = top.reshape(TILE, ROWS, 128)

        def some(i, _):
            for u in range(3):
                one(i * 3 + u)
            return 0

        lax.fori_loop(0, TILES // 3, some, 0)

    def query_first(_):
        query_copy(1).wait_recv()
        step_part(1, ret_out, stat_out)
        for copy in back_copy(1):
            copy.start()

    load_pages.wait()
    step_part(0, ret_in, stat_in)
    lax.fori_loop(0, TILES, new_part, 0)
    ring_step(1)
    lax.fori_loop(5, 11, send_near, 0)
    ring_step(2)
    lax.fori_loop(11, 15, send_near, 0)
    query_first(0)
    ring_step(3)
    lax.fori_loop(1, 5, serve, 0)
    ring_step(4)
    lax.fori_loop(5, 9, serve, 0)
    lax.fori_loop(9, 15, serve, 0)
    x_copy(0).wait_recv()
    prompt_part(0)
    for i in (1, 2):
        x_copy(i).wait_recv()
    prompt_part(1)
    for i in (3, 4):
        x_copy(i).wait_recv()
    prompt_part(2)
    for i in (5, 6):
        x_copy(i).wait_recv()
    prompt_part(3)
    x_copy(7).wait_recv()
    prompt_part(4)

    def settle(t, _):
        sums = acc[pl.ds(t * TILE, TILE)]
        total = sums[:, :, HEAD:]
        acc[pl.ds(t * TILE, TILE), :, :HEAD] = sums[:, :, :HEAD] / total
        high[pl.ds(t * TILE, TILE)] = high[pl.ds(t * TILE, TILE)] + jnp.log2(total)
        return 0

    lax.fori_loop(0, TILES, settle, 0)

    def await_back(o, _):
        for copy in back_copy(o):
            copy.wait_recv()
        return 0

    lax.fori_loop(1, HOLD, await_back, 0)

    lane_of = iota((ROWS, 128), 1) - iota((ROWS, 128), 0)

    head_of = iota((ROWS, 128), 0) >> 2
    weights = jnp.zeros((ROWS, 128), F32)
    for j in range(8):
        weights = jnp.where(head_of == j, w_ref[j:j + 1, :], weights)

    def finish(i, _):
        for u in range(8):
            b = i * 8 + u
            a = tab[ARRIVAL, b] & (HOLD * CAP - 1)
            place = jnp.clip(tab[PLACE, b], 0, PLACES - 1)
            line = stat_in[a >> 3, pl.ds((a >> 2) & 1, 1), :]
            level = jnp.sum(jnp.where(lane_of == (a & 3) * ROWS, line, 0.0), axis=1, keepdims=True)
            mine = 1.0 / (1.0 + jnp.exp2(level - high[place]))
            theirs = ret_in[a].astype(F32)
            result = (theirs + (acc[place, :, :HEAD] - theirs) * mine).astype(BF16)
            out_ref[b] = result
            part[pl.ds(b, 1), :] = jnp.sum(result.astype(F32) * weights, axis=0, keepdims=True)
        return 0

    lax.fori_loop(0, BEAMS // 8, finish, 0)

    score = jnp.sum(part[...], axis=1, keepdims=True)
    spot = iota((BEAMS, 128), 0) == iota((BEAMS, 128), 1)
    line = jnp.sum(jnp.where(spot, score, 0.0), axis=0, keepdims=True) * 0.25
    share[...] = jnp.broadcast_to(line, (8, 128))
    if groups > 1:
        steps = [(g, h, y) for h in (1, 0) for y in (2, 1, 3, 0) for g in (1, 0) if (g, h, y) != (0, 0, 0)]
        if (groups, lanes_tp) != (16, 8):
            steps = None

        def share_copy(i):
            if steps is None:
                to = group_peer(i)
            else:
                g, h, y = steps[i - 1]
                to = {
                    "grp": lax.rem(grp + g, 2),
                    "tp": lax.rem(lax.div(tp, 4) + h, 2) * 4 + lax.rem(lax.rem(tp, 4) + y, 4)}
            return pltpu.make_async_remote_copy(
                src_ref=share, dst_ref=shares.at[group], send_sem=c_ss.at[i], recv_sem=c_rs.at[i],
                device_id=to, device_id_type=MESH)

        share_copies = [share_copy(i) for i in range(1, groups)]
        for copy in share_copies:
            copy.start()
        shares[group] = share[...]
        for copy in share_copies:
            copy.wait()
        score_ref[...] = jnp.sum(shares[...], axis=0)
    else:
        score_ref[...] = share[...]

    def await_sends(o, _):
        query_copy(o).wait_send()
        for copy in back_copy(o):
            copy.wait_send()
        return 0

    lax.fori_loop(1, HOLD, await_sends, 0)
    for s in (1, 2, 3, 4):
        fwd_copy(s).wait_send()
        bwd_copy(s).wait_send()
    for i in range(8):
        x_copy(i).wait_send()


def on_device(queries, new_kv, prompt_key_value, step_key_value, parent_dev, parent_slot, cache_len, prompt_ids, score_weights):
    lanes_tp = lax.axis_size("tp")
    groups = lax.axis_size("grp") * lanes_tp
    vmem = pl.BlockSpec(memory_space=pltpu.VMEM)
    hbm = pl.BlockSpec(memory_space=pltpu.HBM)
    q = queries.reshape(BEAMS, 4, 8, HEAD).transpose(0, 2, 1, 3).reshape(BEAMS, ROWS, HEAD)
    kvn = new_kv.reshape(BEAMS, 4, 2, HEAD).transpose(0, 2, 1, 3).reshape(BEAMS, NEW, HEAD)
    weights = score_weights.reshape(8, HEAD)
    dma = pltpu.SemaphoreType.DMA
    attended, score = pl.pallas_call(
        functools.partial(main_kernel, groups, lanes_tp),
        out_shape=(
            jax.ShapeDtypeStruct((BEAMS, ROWS, HEAD), BF16),
            jax.ShapeDtypeStruct((8, 128), F32),
        ),
        in_specs=[hbm] * 9,
        out_specs=(vmem, vmem),
        scratch_shapes=[
            pltpu.VMEM((8, 128), I32),
            pltpu.VMEM((8, 128), I32),
            pltpu.VMEM((8, 128), I32),
            pltpu.VMEM((1, BEAMS), I32),
            pltpu.VMEM((8, HEAD), F32),
            pltpu.VMEM((TAB, 128), I32),
            pltpu.SMEM((TAB, 128), I32),
            pltpu.VMEM((BEAMS, ROWS, HEAD), BF16),
            pltpu.VMEM((BEAMS, NEW, HEAD), BF16),
            pltpu.VMEM((BEAMS, 128, 2 * HEAD), BF16),
        ] + [pltpu.VMEM((n, 2, SHARD, 2 * HEAD), BF16) for n in (4, 4, 4, 3, 1)] + [
            pltpu.VMEM((HOLD * CAP, ROWS, HEAD), BF16),
            pltpu.VMEM((HOLD * CAP, ROWS, HEAD), BF16),
            pltpu.VMEM((HOLD * CAP, ROWS, HEAD), BF16),
            pltpu.VMEM((HOLD * CAP, ROWS, HEAD), BF16),
            pltpu.VMEM((HOLD, 2, 128), F32),
            pltpu.VMEM((HOLD, 2, 128), F32),
            pltpu.VMEM((PLACES, ROWS, HEAD), BF16),
            pltpu.VMEM((PLACES, NEW, HEAD), F32),
            pltpu.VMEM((PLACES, ROWS, 2 * HEAD), F32),
            pltpu.VMEM((PLACES, ROWS, 128), F32),
            pltpu.VMEM((BEAMS, 128), F32),
            pltpu.VMEM((8, 128), F32),
            pltpu.VMEM((max(groups, 1), 8, 128), F32),
        ] + [dma((HOLD,))] * 6 + [dma((5,))] * 4 + [dma((8,))] * 2 + [dma((max(groups, 1),))] * 2 + [dma((10,))],
        compiler_params=pltpu.CompilerParams(
            collective_id=0, has_side_effects=True, vmem_limit_bytes=VMEM_LIMIT),
    )(parent_dev.reshape(8, 128), parent_slot.reshape(8, 128), cache_len.reshape(8, 128), prompt_ids.reshape(1, BEAMS),
      weights, q, kvn, prompt_key_value[0], step_key_value[0])
    attended = attended.reshape(BEAMS, 8, 4, HEAD).transpose(0, 2, 1, 3)
    return attended.reshape(1, BEAMS, 4, 8 * HEAD), score[0, :BEAMS]


def solution(mesh):
    in_specs = (
        P("grp", "beam", None, "tp"),
        P("grp", "beam", None, "tp"),
        P("grp", None, "beam", "tp"),
        P("grp", "beam", None, "tp"),
        P(),
        P(),
        P(),
        P("beam"),
        P("grp", "tp"),
    )
    out_specs = (P("grp", "beam", None, "tp"), P("beam"))
    return jax.shard_map(on_device, mesh=mesh, in_specs=in_specs, out_specs=out_specs, check_vma=False)
```

```python
import functools
import math

import jax
import jax.numpy as jnp
from jax import lax
from jax.experimental import pallas as pl
from jax.experimental.pallas import tpu as pltpu
from jax.sharding import PartitionSpec as P

MESH = pl.DeviceIdType.MESH
F32, BF16, I32 = jnp.float32, jnp.bfloat16, jnp.int32

HEAD = 128
BEAMS = 64
ROWS = 32
CAP = 8
HOLD = 16
TILE = 8
TILES = BEAMS // TILE + 1
PLACES = TILES * TILE
TROWS = TILE * ROWS
SHARD = 256
NEW = 8
SCALE = math.log2(math.e) / math.sqrt(HEAD)
LOW = -1e30
VMEM_LIMIT = 61 * 1024 * 1024
TAB = 32
INV, PLACED, PROMPT, ARRIVAL, PLACE = 8, 24, 25, 26, 27


def iota(shape, axis):
    return lax.broadcasted_iota(I32, shape, axis)


def make_table(pdev_ref, slot_ref, length_ref, pid_ref, tab_ref):
    me = lax.axis_index("beam")
    z, x = lax.div(me, 2), lax.rem(me, 2)
    pdev = pdev_ref[...]
    code = (slot_ref[...] * 256 + length_ref[...]).astype(F32)

    a, b = iota((128, 128), 0), iota((128, 128), 1)
    upper = ((a < b) & ((a >> 6) == (b >> 6))).astype(F32)
    served = (pdev == me).astype(F32)
    rank = jnp.dot(served, upper, preferred_element_type=F32)
    lane = iota((8, 128), 1)
    head = jnp.zeros((8, 128), F32)
    for k in range(CAP):
        pick = jnp.where(rank == k, served, 0.0) * code
        for h in range(2):
            found = jnp.sum(jnp.where((lane >> 6) == h, pick, 0.0), axis=1, keepdims=True)
            head = jnp.where(lane == h * CAP + k, found, head)
    tab_ref[0:8, :] = head.astype(I32)

    upper = upper[:BEAMS, :BEAMS]
    pair = pdev_ref[pl.ds(z, 1), :]
    mine = jnp.where(x == 1, pair[:, BEAMS:], pair[:, :BEAMS])
    ahead = (((mine >> 1) - z) & 7) * 2 + ((mine - x) & 1)
    offset = iota((HOLD, BEAMS), 0)
    beam = iota((HOLD, BEAMS), 1).astype(F32)
    own = (jnp.broadcast_to(ahead, (HOLD, BEAMS)) == offset).astype(F32)
    own_rank = jnp.dot(own, upper, preferred_element_type=F32)
    lane = iota((HOLD, 128), 1)
    body = jnp.zeros((HOLD, 128), F32)
    for k in range(CAP):
        found = jnp.sum(jnp.where(own_rank == k, own, 0.0) * beam, axis=1, keepdims=True)
        body = jnp.where(lane == k, found, body)
    tab_ref[8:8 + HOLD, :] = body.astype(I32)

    arrival = jnp.sum(own * (offset.astype(F32) * CAP + jnp.minimum(own_rank, CAP - 1)), axis=0, keepdims=True)
    first = (pid_ref[...] == 0).astype(F32)
    before = jnp.dot(jnp.broadcast_to(first, (8, BEAMS)), upper, preferred_element_type=F32)[0:1]
    count = jnp.sum(first, axis=1, keepdims=True).astype(I32)
    filled = (count + (TILE - 1)) & (-TILE)
    after = filled.astype(F32) + iota((1, BEAMS), 1).astype(F32) - before
    place = jnp.where(first > 0.5, before, after)
    diagonal = iota((BEAMS, BEAMS), 0) == iota((BEAMS, BEAMS), 1)
    column = jnp.sum(jnp.where(diagonal, place, 0.0), axis=1, keepdims=True)
    there = column == iota((BEAMS, 128), 1).astype(F32)
    holder = jnp.sum(jnp.where(there, iota((BEAMS, 128), 0).astype(F32), 0.0), axis=0, keepdims=True)
    which = (iota((1, 128), 1) * TILE >= filled).astype(F32)
    rest = jnp.zeros((1, 128 - BEAMS), F32)
    tail = jnp.concatenate([
        holder, which, jnp.concatenate([arrival, rest], axis=1), jnp.concatenate([place, rest], axis=1),
        jnp.zeros((4, 128), F32)], axis=0)
    tab_ref[24:32, :] = tail.astype(I32)


OWN, XOWN, ANTI, XANTI = 0, 1, 14, 15
FWD = {1: 2, 2: 6, 3: 10}
BWD = {1: 3, 2: 7, 3: 11}
XFWD = {1: 4, 2: 8, 3: 12}
XBWD = {1: 5, 2: 9, 3: 13}


def dot_nt(a, b):
    return lax.dot_general(a, b, (((1,), (1,)), ((), ())), preferred_element_type=F32)


def dot_nn(a, b):
    return lax.dot_general(a, b, (((1,), (0,)), ((), ())), preferred_element_type=F32)


def main_kernel(
    groups, lanes_tp, pdev_hbm, slot_hbm, length_hbm, pid_hbm, w_hbm, q_hbm, kvn_hbm, prompt_hbm, pages_hbm,
    out_ref, score_ref,
    pdev_ref, slot_ref, length_ref, pid_ref, w_ref, table, tab, q_ref, kvn_ref, pages, kv0, kv1, kv2, kv3, kv4, send, recv, ret_out, ret_in, stat_out, stat_in,
    qt, kvt, acc, high, part, share, shares,
    q_ss, q_rs, r_ss, r_rs, s_ss, s_rs, f_ss, f_rs, b_ss, b_rs, x_ss, x_rs, c_ss, c_rs, l_sem,
):
    me = lax.axis_index("beam")
    grp = lax.axis_index("grp")
    tp = lax.axis_index("tp")
    group = grp * lanes_tp + tp
    z, x = lax.div(me, 2), lax.rem(me, 2)

    def at(dz, dx):
        return lax.rem(z + dz + 8, 8) * 2 + lax.rem(x + dx, 2)

    def target(o):
        return at(lax.div(o, 2), lax.rem(o, 2))

    def origin(o):
        return at(-lax.div(o, 2), lax.rem(o, 2))

    def near(i):
        g, r = lax.div(i - 1, 4), lax.rem(i - 1, 4)
        return (g + 1 + lax.div(r, 2) * (6 - 2 * g)) * 2 + lax.rem(r, 2)

    up, down, side = at(1, 0), at(-1, 0), at(0, 1)

    held = (kv0, kv1, kv2, kv3, kv4)

    def shard_at(slot):
        if slot == XANTI:
            return kv4.at[0]
        return held[slot // 4].at[slot % 4]

    load_prompt = pltpu.make_async_copy(prompt_hbm, shard_at(OWN), l_sem.at[0])
    load_pages = pltpu.make_async_copy(pages_hbm, pages, l_sem.at[1])
    load_queries = pltpu.make_async_copy(q_hbm, q_ref, l_sem.at[3])
    load_new = pltpu.make_async_copy(kvn_hbm, kvn_ref, l_sem.at[4])
    load_small = [
        pltpu.make_async_copy(src, dst, l_sem.at[5 + i])
        for i, (src, dst) in enumerate((
            (pdev_hbm, pdev_ref), (slot_hbm, slot_ref), (length_hbm, length_ref), (pid_hbm, pid_ref), (w_hbm, w_ref)))]
    load_prompt.start()

    barrier = pltpu.get_barrier_semaphore()

    def greet_beam(o, _):
        pl.semaphore_signal(barrier, inc=1, device_id={"beam": lax.rem(me + o, HOLD)}, device_id_type=MESH)
        return 0

    lax.fori_loop(1, HOLD, greet_beam, 0)

    def group_peer(o):
        peer = lax.rem(group + o, groups)
        return {"grp": lax.div(peer, lanes_tp), "tp": lax.rem(peer, lanes_tp)}

    if groups > 1:
        def greet_group(o, _):
            pl.semaphore_signal(barrier, inc=1, device_id=group_peer(o), device_id_type=MESH)
            return 0

        lax.fori_loop(1, groups, greet_group, 0)

    def shard_copy(src, dst, to, ss, rs, half=None):
        a, b = shard_at(src), shard_at(dst)
        if half is not None:
            a, b = a.at[half], b.at[half]
        return pltpu.make_async_remote_copy(
            src_ref=a, dst_ref=b, send_sem=ss, recv_sem=rs, device_id={"beam": to}, device_id_type=MESH)

    def fwd_copy(s):
        src = OWN if s == 1 else FWD[s - 1]
        if s == 4:
            return shard_copy(src, ANTI, up, f_ss.at[s], f_rs.at[s], 0)
        return shard_copy(src, FWD[s], up, f_ss.at[s], f_rs.at[s])

    def bwd_copy(s):
        src = OWN if s == 1 else BWD[s - 1]
        if s == 4:
            return shard_copy(src, ANTI, down, b_ss.at[s], b_rs.at[s], 1)
        return shard_copy(src, BWD[s], down, b_ss.at[s], b_rs.at[s])

    x_plan = [(OWN, XOWN)]
    for s in (1, 2, 3):
        x_plan += [(FWD[s], XFWD[s]), (BWD[s], XBWD[s])]
    x_plan += [(ANTI, XANTI)]

    def x_copy(i):
        src, dst = x_plan[i]
        return shard_copy(src, dst, side, x_ss.at[i], x_rs.at[i])

    def x_last(half):
        return shard_copy(ANTI, XANTI, side, x_ss.at[7 + half], x_rs.at[7 + half], half)

    for load in load_small + [load_queries, load_new, load_pages]:
        load.start()
    load_prompt.wait()
    pl.semaphore_wait(barrier, HOLD - 1 + groups - 1)
    fwd_copy(1).start()
    bwd_copy(1).start()
    x_copy(0).start()

    for load in load_small:
        load.wait()
    make_table(pdev_ref, slot_ref, length_ref, pid_ref, table)
    load_table = pltpu.make_async_copy(table, tab, l_sem.at[2])
    load_table.start()
    load_table.wait()

    load_queries.wait()
    def span(o):
        return pl.ds(o * CAP, CAP)

    def pack(o, into):
        for k in range(CAP):
            into[o * CAP + k] = q_ref[tab[INV + o, k] & (BEAMS - 1)]


    def query_copy(o):
        return pltpu.make_async_remote_copy(
            src_ref=send.at[span(o)], dst_ref=recv.at[span(o)], send_sem=q_ss.at[o], recv_sem=q_rs.at[o],
            device_id={"beam": target(o)}, device_id_type=MESH)

    def send_near(i, _):
        o = near(i)
        pack(o, send)
        query_copy(o).start()
        return 0

    pack(1, send)
    query_copy(1).start()
    lax.fori_loop(1, 5, send_near, 0)
    pack(0, recv)
    load_new.wait()

    def ring_step(s):
        fwd_copy(s).wait_recv()
        if s < 4:
            fwd_copy(s + 1).start()
            x_copy(2 * s - 1).start()
        else:
            x_last(0).start()
        bwd_copy(s).wait_recv()
        if s < 4:
            bwd_copy(s + 1).start()
            x_copy(2 * s).start()
        else:
            x_last(1).start()

    def fill_tile(t, _):
        for i in range(TILE):
            b = tab[PLACED, t * TILE + i] & (BEAMS - 1)
            qt[t * TILE + i] = q_ref[b]
            kvt[t * TILE + i] = kvn_ref[b].astype(F32)
        return 0

    lax.fori_loop(0, TILES, fill_tile, 0)

    def with_ones(values):
        return jnp.concatenate([values, jnp.ones(values.shape, BF16)], axis=1)

    diag = (iota((TROWS, 128), 0) & 127) == iota((TROWS, 128), 1)
    column = iota((ROWS, 128), 1)

    def step_part(o, into_out, into_stat):
        c = origin(o)
        row, lane = lax.div(c, 2), lax.rem(c, 2) * CAP
        blocks = []
        values = []
        for j in range(CAP // 2):
            k0 = 2 * j
            code0, code1 = tab[row, lane + k0], tab[row, lane + k0 + 1]
            page0, page1 = pages[(code0 >> 8) & (BEAMS - 1)], pages[(code1 >> 8) & (BEAMS - 1)]
            keys = jnp.concatenate([page0[:, :HEAD], page1[:, :HEAD]], axis=0)
            values.append(with_ones(jnp.concatenate([page0[:, HEAD:], page1[:, HEAD:]], axis=0)))
            queries = recv[pl.ds(o * CAP + k0, 2)].reshape(2 * ROWS, HEAD)
            s = dot_nt(queries, keys)
            blocks.append(jnp.where(column < (code0 & 255), s[:ROWS, :128] * SCALE, LOW))
            blocks.append(jnp.where(column < (code1 & 255), s[ROWS:, 128:] * SCALE, LOW))
        s = jnp.concatenate(blocks, axis=0)
        top = jnp.max(s, axis=1, keepdims=True)
        p = jnp.exp2(s - top).astype(BF16)
        zero = jnp.zeros((ROWS, 128), BF16)
        sums = []
        for j in range(CAP // 2):
            p0, p1 = p[2 * j * ROWS:(2 * j + 1) * ROWS], p[(2 * j + 1) * ROWS:(2 * j + 2) * ROWS]
            wide = jnp.concatenate(
                [jnp.concatenate([p0, zero], axis=1), jnp.concatenate([zero, p1], axis=1)], axis=0)
            sums.append(dot_nn(wide, values[j]))
        sums = jnp.concatenate(sums, axis=0)
        total = sums[:, HEAD:]
        into_out[span(o)] = (sums[:, :HEAD] / total).astype(BF16).reshape(CAP, ROWS, HEAD)
        level = top + jnp.log2(total)
        flat = jnp.sum(jnp.where(diag, level, 0.0).reshape(2, 128, 128), axis=1)
        into_stat[o] = flat

    def back_copy(o):
        to = {"beam": origin(o)}
        return (
            pltpu.make_async_remote_copy(
                src_ref=ret_out.at[span(o)], dst_ref=ret_in.at[span(o)], send_sem=r_ss.at[o],
                recv_sem=r_rs.at[o], device_id=to, device_id_type=MESH),
            pltpu.make_async_remote_copy(
                src_ref=stat_out.at[o], dst_ref=stat_in.at[o], send_sem=s_ss.at[o],
                recv_sem=s_rs.at[o], device_id=to, device_id_type=MESH),
        )

    def serve(i, _):
        o = near(i)
        query_copy(o).wait_recv()
        step_part(o, ret_out, stat_out)
        for copy in back_copy(o):
            copy.start()
        return 0

    def new_part(t, _):
        q = qt[pl.ds(t * TILE, TILE)].reshape(TROWS, HEAD)
        kv = kvt[pl.ds(t * TILE, TILE)].reshape(TILE * NEW, HEAD)
        kv = jnp.concatenate([kv, jnp.zeros(kv.shape, F32)], axis=0).astype(BF16)
        row, col = iota((TROWS, 128), 0), iota((TROWS, 128), 1)
        seen = ((row >> 5) == (col >> 3)) & ((col & 7) <= (row & 3))
        s = jnp.where(seen, dot_nt(q, kv) * SCALE, LOW)
        top = jnp.max(s, axis=1, keepdims=True)
        p = pltpu.roll(jnp.exp2(s - top), 4, 1).astype(BF16)
        acc[pl.ds(t * TILE, TILE)] = dot_nn(p, with_ones(kv)).reshape(TILE, ROWS, 2 * HEAD)
        high[pl.ds(t * TILE, TILE)] = jnp.broadcast_to(top, (TROWS, 128)).reshape(TILE, ROWS, 128)
        return 0

    def prompt_part(number):
        keys = held[number].shape[0] * SHARD

        def one(t):
            own = tab[PROMPT, t] & 1
            q = qt[pl.ds(t * TILE, TILE)].reshape(TROWS, HEAD)
            kv = held[number][:, own].reshape(keys, 2 * HEAD)
            s = dot_nt(q, kv[:, :HEAD])
            cols = [s[:, i * 128:(i + 1) * 128] for i in range(keys // 128)]
            top = functools.reduce(jnp.maximum, cols)
            old = high[pl.ds(t * TILE, TILE)].reshape(TROWS, 128)
            top = jnp.maximum(old, jnp.max(top, axis=1, keepdims=True) * SCALE)
            p = jnp.concatenate([jnp.exp2(col * SCALE - top).astype(BF16) for col in cols], axis=1)
            fade = jnp.exp2(old - top)
            add = dot_nn(p, with_ones(kv[:, HEAD:]))
            was = acc[pl.ds(t * TILE, TILE)].reshape(TROWS, 2 * HEAD)
            new = was * jnp.concatenate([fade, fade], axis=1) + add
            acc[pl.ds(t * TILE, TILE)] = new.reshape(TILE, ROWS, 2 * HEAD)
            high[pl.ds(t * TILE, TILE)] = top.reshape(TILE, ROWS, 128)

        def some(i, _):
            for u in range(3):
                one(i * 3 + u)
            return 0

        lax.fori_loop(0, TILES // 3, some, 0)

    def query_first(_):
        query_copy(1).wait_recv()
        step_part(1, ret_out, stat_out)
        for copy in back_copy(1):
            copy.start()

    load_pages.wait()
    step_part(0, ret_in, stat_in)
    lax.fori_loop(0, TILES, new_part, 0)
    ring_step(1)
    lax.fori_loop(5, 11, send_near, 0)
    ring_step(2)
    lax.fori_loop(11, 15, send_near, 0)
    query_first(0)
    ring_step(3)
    lax.fori_loop(1, 5, serve, 0)
    ring_step(4)
    lax.fori_loop(5, 9, serve, 0)
    lax.fori_loop(9, 15, serve, 0)
    x_copy(0).wait_recv()
    prompt_part(0)
    for i in (1, 2):
        x_copy(i).wait_recv()
    prompt_part(1)
    for i in (3, 4):
        x_copy(i).wait_recv()
    prompt_part(2)
    for i in (5, 6):
        x_copy(i).wait_recv()
    prompt_part(3)
    for half in (0, 1):
        x_last(half).wait_recv()
    prompt_part(4)

    def settle(t, _):
        sums = acc[pl.ds(t * TILE, TILE)]
        total = sums[:, :, HEAD:]
        acc[pl.ds(t * TILE, TILE), :, :HEAD] = sums[:, :, :HEAD] / total
        high[pl.ds(t * TILE, TILE)] = high[pl.ds(t * TILE, TILE)] + jnp.log2(total)
        return 0

    lax.fori_loop(0, TILES, settle, 0)

    def await_back(o, _):
        for copy in back_copy(o):
            copy.wait_recv()
        return 0

    lax.fori_loop(1, HOLD, await_back, 0)

    lane_of = iota((ROWS, 128), 1) - iota((ROWS, 128), 0)

    head_of = iota((ROWS, 128), 0) >> 2
    weights = jnp.zeros((ROWS, 128), F32)
    for j in range(8):
        weights = jnp.where(head_of == j, w_ref[j:j + 1, :], weights)

    def finish(i, _):
        for u in range(8):
            b = i * 8 + u
            a = tab[ARRIVAL, b] & (HOLD * CAP - 1)
            place = jnp.clip(tab[PLACE, b], 0, PLACES - 1)
            line = stat_in[a >> 3, pl.ds((a >> 2) & 1, 1), :]
            level = jnp.sum(jnp.where(lane_of == (a & 3) * ROWS, line, 0.0), axis=1, keepdims=True)
            mine = 1.0 / (1.0 + jnp.exp2(level - high[place]))
            theirs = ret_in[a].astype(F32)
            result = (theirs + (acc[place, :, :HEAD] - theirs) * mine).astype(BF16)
            out_ref[b] = result
            part[pl.ds(b, 1), :] = jnp.sum(result.astype(F32) * weights, axis=0, keepdims=True)
        return 0

    lax.fori_loop(0, BEAMS // 8, finish, 0)

    score = jnp.sum(part[...], axis=1, keepdims=True)
    spot = iota((BEAMS, 128), 0) == iota((BEAMS, 128), 1)
    line = jnp.sum(jnp.where(spot, score, 0.0), axis=0, keepdims=True) * 0.25
    share[...] = jnp.broadcast_to(line, (8, 128))
    if groups > 1:
        steps = [(g, h, y) for h in (1, 0) for y in (2, 1, 3, 0) for g in (1, 0) if (g, h, y) != (0, 0, 0)]
        if (groups, lanes_tp) != (16, 8):
            steps = None

        def share_copy(i):
            if steps is None:
                to = group_peer(i)
            else:
                g, h, y = steps[i - 1]
                to = {
                    "grp": lax.rem(grp + g, 2),
                    "tp": lax.rem(lax.div(tp, 4) + h, 2) * 4 + lax.rem(lax.rem(tp, 4) + y, 4)}
            return pltpu.make_async_remote_copy(
                src_ref=share, dst_ref=shares.at[group], send_sem=c_ss.at[i], recv_sem=c_rs.at[i],
                device_id=to, device_id_type=MESH)

        share_copies = [share_copy(i) for i in range(1, groups)]
        for copy in share_copies:
            copy.start()
        shares[group] = share[...]
        for copy in share_copies:
            copy.wait()
        score_ref[...] = jnp.sum(shares[...], axis=0)
    else:
        score_ref[...] = share[...]

    def await_sends(o, _):
        query_copy(o).wait_send()
        for copy in back_copy(o):
            copy.wait_send()
        return 0

    lax.fori_loop(1, HOLD, await_sends, 0)
    for s in (1, 2, 3, 4):
        fwd_copy(s).wait_send()
        bwd_copy(s).wait_send()
    for i in range(7):
        x_copy(i).wait_send()
    for half in (0, 1):
        x_last(half).wait_send()


def on_device(queries, new_kv, prompt_key_value, step_key_value, parent_dev, parent_slot, cache_len, prompt_ids, score_weights):
    lanes_tp = lax.axis_size("tp")
    groups = lax.axis_size("grp") * lanes_tp
    vmem = pl.BlockSpec(memory_space=pltpu.VMEM)
    hbm = pl.BlockSpec(memory_space=pltpu.HBM)
    q = queries.reshape(BEAMS, 4, 8, HEAD).transpose(0, 2, 1, 3).reshape(BEAMS, ROWS, HEAD)
    kvn = new_kv.reshape(BEAMS, 4, 2, HEAD).transpose(0, 2, 1, 3).reshape(BEAMS, NEW, HEAD)
    weights = score_weights.reshape(8, HEAD)
    dma = pltpu.SemaphoreType.DMA
    attended, score = pl.pallas_call(
        functools.partial(main_kernel, groups, lanes_tp),
        out_shape=(
            jax.ShapeDtypeStruct((BEAMS, ROWS, HEAD), BF16),
            jax.ShapeDtypeStruct((8, 128), F32),
        ),
        in_specs=[hbm] * 9,
        out_specs=(vmem, vmem),
        scratch_shapes=[
            pltpu.VMEM((8, 128), I32),
            pltpu.VMEM((8, 128), I32),
            pltpu.VMEM((8, 128), I32),
            pltpu.VMEM((1, BEAMS), I32),
            pltpu.VMEM((8, HEAD), F32),
            pltpu.VMEM((TAB, 128), I32),
            pltpu.SMEM((TAB, 128), I32),
            pltpu.VMEM((BEAMS, ROWS, HEAD), BF16),
            pltpu.VMEM((BEAMS, NEW, HEAD), BF16),
            pltpu.VMEM((BEAMS, 128, 2 * HEAD), BF16),
        ] + [pltpu.VMEM((n, 2, SHARD, 2 * HEAD), BF16) for n in (4, 4, 4, 3, 1)] + [
            pltpu.VMEM((HOLD * CAP, ROWS, HEAD), BF16),
            pltpu.VMEM((HOLD * CAP, ROWS, HEAD), BF16),
            pltpu.VMEM((HOLD * CAP, ROWS, HEAD), BF16),
            pltpu.VMEM((HOLD * CAP, ROWS, HEAD), BF16),
            pltpu.VMEM((HOLD, 2, 128), F32),
            pltpu.VMEM((HOLD, 2, 128), F32),
            pltpu.VMEM((PLACES, ROWS, HEAD), BF16),
            pltpu.VMEM((PLACES, NEW, HEAD), F32),
            pltpu.VMEM((PLACES, ROWS, 2 * HEAD), F32),
            pltpu.VMEM((PLACES, ROWS, 128), F32),
            pltpu.VMEM((BEAMS, 128), F32),
            pltpu.VMEM((8, 128), F32),
            pltpu.VMEM((max(groups, 1), 8, 128), F32),
        ] + [dma((HOLD,))] * 6 + [dma((5,))] * 4 + [dma((9,))] * 2 + [dma((max(groups, 1),))] * 2 + [dma((10,))],
        compiler_params=pltpu.CompilerParams(
            collective_id=0, has_side_effects=True, vmem_limit_bytes=VMEM_LIMIT),
    )(parent_dev.reshape(8, 128), parent_slot.reshape(8, 128), cache_len.reshape(8, 128), prompt_ids.reshape(1, BEAMS),
      weights, q, kvn, prompt_key_value[0], step_key_value[0])
    attended = attended.reshape(BEAMS, 8, 4, HEAD).transpose(0, 2, 1, 3)
    return attended.reshape(1, BEAMS, 4, 8 * HEAD), score[0, :BEAMS]


def solution(mesh):
    in_specs = (
        P("grp", "beam", None, "tp"),
        P("grp", "beam", None, "tp"),
        P("grp", None, "beam", "tp"),
        P("grp", "beam", None, "tp"),
        P(),
        P(),
        P(),
        P("beam"),
        P("grp", "tp"),
    )
    out_specs = (P("grp", "beam", None, "tp"), P("beam"))
    return jax.shard_map(on_device, mesh=mesh, in_specs=in_specs, out_specs=out_specs, check_vma=False)
```
